32 devices in a mesh: rep: 8 (over y, x, core), shard: 4 (over z).
Axes of the slice: x: 2, y: 2, z: 4, core: 2. Of those that a mesh axis runs over, the one named last changes fastest.
Arguments:
- hidden_in: bfloat16 [8192, 1600], P(('rep', 'shard'))
- cotangent: bfloat16 [8192, 1600], P(('rep', 'shard')), may hold values from -6 to 6
- slot_index: int32 [8192], P('rep'), may hold values from 0 to 1023, as said below
- seq_lengths: int32 [8, 2], P('rep'), may hold values from 384 to 640, as said below
- attn_gain: bfloat16 [1600], P('shard'), may hold values from 0.5 to 1.5
- attn_shift: bfloat16 [1600], P('shard'), may hold values from -4 to 4
- attn_weight: bfloat16 [1600, 4800], P('shard'), may hold values from -0.15625 to 0.15625
- query_bias: bfloat16 [1600], P('shard'), may hold values from -4 to 4
- value_bias: bfloat16 [1600], P('shard'), may hold values from -0.3125 to 0.3125
- out_weight: bfloat16 [1600, 1600], P('shard'), may hold values from -3 to 3
- out_bias: bfloat16 [1600], P('shard'), may hold values from -4 to 4
- mlp_gain: bfloat16 [1600], P('shard'), may hold values from 0.5 to 1.5
- mlp_shift: bfloat16 [1600], P('shard'), may hold values from -4 to 4
- up_weight: bfloat16 [1600, 6400], P('shard'), may hold values from -0.15625 to 0.15625
- up_bias: bfloat16 [6400], P('shard'), may hold values from -4 to 4
- down_weight: bfloat16 [6400, 1600], P('shard'), may hold values from -0.078125 to 0.078125
- down_bias: bfloat16 [1600], P('shard'), may hold values from -4 to 4
Outputs:
- block_out: bfloat16 [8192, 1600], P(('rep', 'shard'))
- input_grad: float32 [8192, 1600], P(('rep', 'shard'))
- grad_attn_gain: float32 [1600], P('shard')
- grad_attn_shift: float32 [1600], P('shard')
- grad_attn_weight: float32 [1600, 4800], P('shard')
- grad_query_bias: float32 [1600], P('shard')
- grad_value_bias: float32 [1600], P('shard')
- grad_out_weight: float32 [1600, 1600], P('shard')
- grad_out_bias: float32 [1600], P('shard')
- grad_mlp_gain: float32 [1600], P('shard')
- grad_mlp_shift: float32 [1600], P('shard')
- grad_up_weight: float32 [1600, 6400], P('shard')
- grad_up_bias: float32 [6400], P('shard')
- grad_down_weight: float32 [6400, 1600], P('shard')
- grad_down_bias: float32 [1600], P('shard')
The draws below stay inside these ranges and needn't reach their ends.
Inputs may be any that keep to these rules, and one draw needn't show every extreme that they name: `slot_index`: within each group (one index of rep), entry s is the place in the group's pack of the token in slot s; the 1024 entries are a permutation that keeps aligned blocks of 128 slots whole and in order. Device k of shard holds slots k * 256 to (k + 1) * 256 - 1 of its group. `seq_lengths`: each row sums to 1024; the longer sequence of a group has min(1024, 512) tokens or more.
All inputs are finite; a program needn't handle non-finite values.
Results may differ from the reference program's by a relative error of at most 0.02.
Values may be sent and summed in bfloat16 or wider, within the bound.
No kernel may reach another device: no remote copies, remote signals or barrier semaphores. Data moves between devices by JAX's collectives and lax.ppermute only.
A program may use at most 384 MiB of HBM per device.

```python
import jax
import jax.numpy as jnp
import numpy as np
from jax import lax

D = 1600
H = 25
FF = 6400
TOK_DEV = 256
MINSEQ = 1024
BLK = 128
GROUP_TOK = 1024
LEAST = 384
REPLICAS = 8
SHARDS = 4
TOKENS = 8192


def draw_hidden_in(key, part):
    key = jax.random.fold_in(key, 37)
    base_key, column_key, row_key = jax.random.split(key, 3)
    column_scale = jnp.exp(jax.random.uniform(column_key, (1, D), jnp.float32, np.log(0.3), np.log(3.0)))
    row_scale = jnp.exp(jax.random.uniform(row_key, (TOKENS, 1), jnp.float32, np.log(0.5), np.log(2.0)))
    base_vals = jax.random.normal(base_key, (TOKENS, D), jnp.float32)
    return (base_vals * column_scale * row_scale).astype(jnp.bfloat16)


def draw_seq_lengths(key, part):
    key = jax.random.fold_in(key, 11)
    length_key, order_key, pick_key = jax.random.split(key, 3)
    longest = GROUP_TOK - LEAST
    shortest_long = min(MINSEQ, longest - BLK)
    long_len = jax.random.randint(length_key, (REPLICAS,), shortest_long, longest + 1)
    chosen = jax.random.randint(pick_key, (), 0, REPLICAS)
    long_len = jnp.where(jnp.arange(REPLICAS) == chosen, longest, long_len)
    long_first = jax.random.randint(order_key, (REPLICAS,), 0, 2)
    first_len = jnp.where(long_first == 1, long_len, GROUP_TOK - long_len)
    return jnp.stack([first_len, GROUP_TOK - first_len], axis=1).astype(jnp.int32)


def draw_slot_index(key, part):
    key = jax.random.fold_in(key, 23)
    per_dev = TOK_DEV // BLK
    block_count = GROUP_TOK // BLK
    special_list = [0, SHARDS // 2 * per_dev, (SHARDS - 1) * per_dev]
    special = np.array(special_list, dtype=np.int32)
    others = np.array([b for b in range(block_count) if b not in special_list], dtype=np.int32)

    def one_group(group_key):
        head_key, rest_key = jax.random.split(group_key)
        head_order = jax.random.permutation(head_key, jnp.arange(3, dtype=jnp.int32))
        rest_order = jax.random.permutation(rest_key, jnp.arange(3, block_count, dtype=jnp.int32))
        owner_block = jnp.zeros((block_count,), jnp.int32).at[special].set(head_order).at[others].set(rest_order)
        return (owner_block[:, None] * BLK + jnp.arange(BLK, dtype=jnp.int32)[None, :]).reshape(-1)
    return jax.vmap(one_group)(jax.random.split(key, REPLICAS)).reshape(-1).astype(jnp.int32)


def block_scale(stream_key, shape, shards, low, top_value):
    factor_of = 1.0
    for dim, blocks in shards:
        steps = jax.random.uniform(jax.random.fold_in(jax.random.fold_in(stream_key, 6), dim), (blocks,), jnp.float32, low / len(shards), top_value / len(shards))
        factor_of = factor_of * jnp.repeat(jnp.exp(steps), shape[dim] // blocks).reshape((-1,) + (1,) * (len(shape) - 1 - dim))
    return factor_of


def gaussian(own_key, dims, width, reach, shards=(), held_as=jnp.bfloat16):
    level = block_scale(own_key, dims, shards, -0.22, 0.18) if shards else 1.0
    entries = jax.random.normal(own_key, dims, jnp.float32) * width * level
    return jnp.minimum(jnp.maximum(entries, -reach), reach).astype(held_as)


def setup_inputs(seed: int = 0) -> dict:
    streams_of = jax.random.split(jax.random.key(seed), 18)
    return {
        "hidden_in": draw_hidden_in(jax.random.fold_in(streams_of[17], 71), 0),
        "cotangent": gaussian(streams_of[1], (TOKENS, D), 1.0, 6.0, ((0, 32),)),
        "slot_index": draw_slot_index(jax.random.fold_in(streams_of[17], 71), 0),
        "seq_lengths": draw_seq_lengths(jax.random.fold_in(streams_of[17], 71), 0),
        "attn_gain": jnp.clip(1.0 + 0.1 * jax.random.normal(streams_of[4], (D,), jnp.float32), 0.5, 1.5).astype(jnp.bfloat16),
        "attn_shift": gaussian(streams_of[5], (D,), 0.3, 4.0, ((0, 4),)),
        "attn_weight": gaussian(streams_of[6], (D, 3 * D), D ** -0.5, 0.15625, ((0, 4),)),
        "query_bias": gaussian(streams_of[7], (D,), 0.3, 4.0, ((0, 4),)),
        "value_bias": gaussian(streams_of[8], (D,), 0.02, 0.3125, ((0, 4),)),
        "out_weight": gaussian(streams_of[9], (D, D), 4 ** -0.5, 3.0, ((0, 4),)),
        "out_bias": gaussian(streams_of[10], (D,), 0.3, 4.0, ((0, 4),)),
        "mlp_gain": jnp.clip(1.0 + 0.1 * jax.random.normal(streams_of[11], (D,), jnp.float32), 0.5, 1.5).astype(jnp.bfloat16),
        "mlp_shift": gaussian(streams_of[12], (D,), 0.3, 4.0, ((0, 4),)),
        "up_weight": gaussian(streams_of[13], (D, FF), D ** -0.5, 0.15625, ((0, 4),)),
        "up_bias": gaussian(streams_of[14], (FF,), 0.5, 4.0, ((0, 4),)),
        "down_weight": gaussian(streams_of[15], (FF, D), FF ** -0.5, 0.078125, ((0, 4),)),
        "down_bias": gaussian(streams_of[16], (D,), 0.3, 4.0, ((0, 4),)),
    }


@jax.custom_vjp
def low(v):
    return lax.optimization_barrier(v.astype(jnp.bfloat16)).astype(jnp.float32)

@jax.custom_vjp
def low_back(v):
    return v

def low_keep(v):
    return (low(v), None)

def low_pass(kept, grad):
    return (grad,)

def back_keep(v):
    return (v, None)

def back_low(kept, grad):
    return (low(grad),)
low.defvjp(low_keep, low_pass)
low_back.defvjp(back_keep, back_low)
EPSILON = 1e-05
HIGHEST = lax.Precision.HIGHEST

def layer_norm(stream, gain_vec, shift_vec):
    average = lax.optimization_barrier(jnp.mean(stream, axis=-1, keepdims=True))
    centred = stream - average
    variance = lax.optimization_barrier(jnp.mean(centred * centred, axis=-1, keepdims=True))
    return centred * lax.rsqrt(variance + EPSILON) * gain_vec + shift_vec

def doc_numbers(pack_ids, seq_sizes):
    ends_at = jnp.cumsum(seq_sizes).astype(jnp.int32)
    return lax.optimization_barrier(jnp.sum((pack_ids[:, None] >= ends_at[None, :]).astype(jnp.int32), axis=1)).astype(jnp.int32)

def group_block(rows_in, pack_ids, seq_sizes, weights):
    attn_gain, attn_shift, attn_weight, query_bias, value_bias, out_weight, out_bias, mlp_gain, mlp_shift, up_weight, up_bias, down_weight, down_bias = weights
    group_size, model_width = rows_in.shape
    head_size = model_width // H
    doc_ids = doc_numbers(pack_ids, seq_sizes)
    normed_a = low(layer_norm(rows_in, attn_gain, attn_shift))
    mixed_rows = jnp.dot(normed_a, attn_weight, precision=HIGHEST)
    queries = low_back(low(mixed_rows[:, :model_width] + query_bias)).reshape(group_size, H, head_size)
    key_rows = low_back(low(mixed_rows[:, model_width:2 * model_width])).reshape(group_size, H, head_size)
    value_rows = low_back(low(mixed_rows[:, 2 * model_width:] + value_bias)).reshape(group_size, H, head_size)
    block_rows = min(512, group_size)
    block_count = group_size // block_rows

    def attend(inputs):
        query_block, pack_block, doc_block = inputs
        scores = low_back(jnp.einsum('thd,khd->htk', query_block, key_rows, precision=HIGHEST) * 0.125)
        visible = (doc_block[:, None] == doc_ids[None, :]) & (pack_ids[None, :] <= pack_block[:, None])
        scores = jnp.where(visible[None], scores, -1000000000.0)
        row_max = lax.optimization_barrier(jnp.max(scores, axis=-1, keepdims=True))
        log_total = row_max + jnp.log(lax.optimization_barrier(jnp.sum(jnp.exp(scores - row_max), axis=-1, keepdims=True)))
        soft_low = low(jnp.exp(scores - log_total))
        return jnp.einsum('htk,khd->thd', soft_low, value_rows, precision=HIGHEST)
    outputs = lax.map(jax.checkpoint(attend), (queries.reshape(block_count, block_rows, H, head_size), pack_ids.reshape(block_count, block_rows), doc_ids.reshape(block_count, block_rows)))
    attended = low_back(low(outputs.reshape(group_size, model_width)))
    branch_a = low_back(jnp.dot(attended, out_weight, precision=HIGHEST) + out_bias)
    middle = rows_in + branch_a
    normed_b = low(layer_norm(middle, mlp_gain, mlp_shift))
    pre_act = low_back(jnp.dot(normed_b, up_weight, precision=HIGHEST) + up_bias)
    act_low = low(jax.nn.gelu(pre_act, approximate=True))
    branch_b = low_back(jnp.dot(act_low, down_weight, precision=HIGHEST) + down_bias)
    return middle + branch_b

def reference(hidden_in, cotangent, slot_index, seq_lengths, attn_gain, attn_shift, attn_weight, query_bias, value_bias, out_weight, out_bias, mlp_gain, mlp_shift, up_weight, up_bias, down_weight, down_bias):
    params = tuple((weight_in.astype(jnp.float32) for weight_in in (attn_gain, attn_shift, attn_weight, query_bias, value_bias, out_weight, out_bias, mlp_gain, mlp_shift, up_weight, up_bias, down_weight, down_bias)))
    stream = hidden_in.astype(jnp.float32)
    slot_groups = slot_index.reshape(REPLICAS, GROUP_TOK)

    def forward(stream_in, *weights):
        grouped = stream_in.reshape(REPLICAS, GROUP_TOK, stream_in.shape[1])

        def step(carried, inputs):
            rows_in, pack_ids, seq_sizes = inputs
            return (carried, jax.checkpoint(group_block)(rows_in, pack_ids, seq_sizes, weights))
        _, outputs = lax.scan(step, jnp.zeros((), jnp.float32), (grouped, slot_groups, seq_lengths))
        return outputs.reshape(stream_in.shape)
    block_out, backward_fn = jax.vjp(forward, stream, *params)
    gradients = backward_fn(cotangent.astype(jnp.float32))
    return (block_out.astype(jnp.bfloat16), gradients[0], gradients[1], gradients[2], gradients[3], gradients[4], gradients[5], gradients[6], gradients[7], gradients[8], gradients[9], gradients[10], gradients[11], gradients[12], gradients[13])
```

```python
import functools

import jax
import jax.numpy as jnp
from jax import lax
from jax.experimental import pallas as pl
from jax.experimental.pallas import tpu as pltpu
from jax.sharding import Mesh
from jax.sharding import PartitionSpec as P

H = 25
BLK = 128
TILE = 256
EPSILON = 1e-05
BF = jnp.bfloat16
F32 = jnp.float32
VMEM_LIMIT = 56 * 1024 * 1024
SMALL_ROWS = 8


def dot_nt(a, b):
    return lax.dot_general(a, b, (((1,), (1,)), ((), ())), preferred_element_type=F32)


def dot_tn(a, b):
    return lax.dot_general(a, b, (((0,), (0,)), ((), ())), preferred_element_type=F32)


def dot_nn(a, b):
    return lax.dot_general(a, b, (((1,), (0,)), ((), ())), preferred_element_type=F32)


def head_plan(shards):
    base, extra = H // shards, H % shards
    counts = [base + (1 if s < extra else 0) for s in range(shards)]
    starts = [sum(counts[:s]) for s in range(shards)]
    width = max(counts)
    windows = [min(st, H - width) for st in starts]
    return counts, starts, windows, width


LONG = 20_000_000_000
SHORT = 10_000_000_000


def call(kernel, scalars, grid, ins, outs, scratch=(), flops=1024):
    return pl.pallas_call(
        kernel,
        out_shape=[jax.ShapeDtypeStruct(shape, dtype) for shape, dtype, _ in outs],
        grid_spec=pltpu.PrefetchScalarGridSpec(
            num_scalar_prefetch=len(scalars),
            grid=grid,
            in_specs=[spec for _, spec in ins],
            out_specs=[spec for _, _, spec in outs],
            scratch_shapes=list(scratch),
        ),
        compiler_params=pltpu.CompilerParams(vmem_limit_bytes=VMEM_LIMIT),
        cost_estimate=pl.CostEstimate(flops=flops, bytes_accessed=1024, transcendentals=0),
    )(*scalars, *[array for array, _ in ins])


def whole(array):
    zeros = (0,) * array.ndim
    return pl.BlockSpec(array.shape, lambda *_: zeros, pipeline_mode=pl.Buffered(1))


def fixed(shape):
    zeros = (0,) * len(shape)
    return pl.BlockSpec(shape, lambda *_: zeros)


def tokens(rows):
    return pl.BlockSpec((rows, TILE), lambda i, *_: (0, i))


def slot_block(rows, per, which):
    return pl.BlockSpec(
        (rows, BLK), lambda i, tab, *_: (tab[2 * i + which] // per, lax.rem(tab[2 * i + which], per))
    )


STEP = 80


def sweep(rows, body, carry, step=STEP):
    while rows % step:
        step -= 16
    for at in range(0, rows, step):
        carry = body(pl.ds(at, step), carry)
    return carry


def chunk(rows, lanes):
    step = STEP
    while rows % step:
        step -= 16
    return jnp.zeros((step, lanes), F32)


def column_mean(acc, rows):
    return jnp.sum(acc, axis=0, keepdims=True) * (1.0 / rows)


def norm_stats(load, rows, lanes):
    zero = chunk(rows, lanes)
    mean = column_mean(sweep(rows, lambda at, acc: acc + load(at), zero), rows)

    def spread(at, acc):
        centred = load(at) - mean
        return acc + centred * centred

    return mean, lax.rsqrt(column_mean(sweep(rows, spread, zero), rows) + EPSILON)


def norm_back(load, load_e, gain_ref, col, rows, lanes, write):
    mean, rstd = norm_stats(load, rows, lanes)
    zero = chunk(rows, lanes)

    def both(at):
        return (load(at) - mean) * rstd, load_e(at) * gain_ref[at, col : col + 1]

    def sums(at, carry):
        x, c = both(at)
        return carry[0] + c, carry[1] + c * x

    mean_c, mean_cx = sweep(rows, sums, (zero, zero))
    mean_c, mean_cx = column_mean(mean_c, rows), column_mean(mean_cx, rows)

    def last(at, carry):
        x, c = both(at)
        write(at, rstd * (c - mean_c - x * mean_cx))
        return carry

    sweep(rows, last, 0)


def slot_places(tab_ref, rows, per):
    places = []
    for which in range(2):
        place = tab_ref[2 * pl.program_id(0) + which]
        row = pl.multiple_of((place // per) * rows, 16)
        places.append((row, pl.multiple_of(lax.rem(place, per) * BLK, BLK)))
    return places


def store_slots(out_ref, places, at, value):
    for which, (row, lane) in enumerate(places):
        rows = pl.ds(pl.multiple_of(row + at.start, 16), at.size)
        out_ref[rows, pl.ds(lane, BLK)] = value[:, which * BLK : (which + 1) * BLK].astype(out_ref.dtype)


def clear_first(*refs):
    @pl.when(pl.program_id(0) == 0)
    def _():
        for ref in refs:
            ref[...] = jnp.zeros_like(ref)


def first_norm_kernel(tab_ref, h0_ref, h1_ref, small_ref, na_ref, pack_ref):
    rows = na_ref.shape[0]
    for j, ref in enumerate((h0_ref, h1_ref)):
        load = lambda at, ref=ref: ref[at, :].astype(F32)
        mean, rstd = norm_stats(load, rows, BLK)

        def write(at, carry, load=load, mean=mean, rstd=rstd, j=j):
            x = (load(at) - mean) * rstd
            na_ref[at, j * BLK : (j + 1) * BLK] = (x * small_ref[at, 0:1] + small_ref[at, 1:2]).astype(BF)
            return carry

        pack_ref[:, j * BLK : (j + 1) * BLK] = ref[...]

        sweep(rows, write, 0)


def first_norm_call(tab, hidden_all, small, shards):
    width, tok = small.shape[0], hidden_all.shape[1]
    group = tok * shards
    per = tok // BLK
    return call(
        first_norm_kernel,
        (tab,),
        (group // TILE,),
        [
            (hidden_all, slot_block(width, per, 0)),
            (hidden_all, slot_block(width, per, 1)),
            (small, whole(small)),
        ],
        [((width, group), BF, tokens(width))] * 2,
        flops=LONG,
    )


def tile_variants(tiles):
    return [(i, st) for i in range(tiles) for st in range(i + 1)]


def allowed_mask(first_len, q_base, k_base, k_rows):
    kpos = k_base + lax.broadcasted_iota(jnp.int32, (k_rows, TILE), 0)
    qrow = q_base + lax.broadcasted_iota(jnp.int32, (1, TILE), 1)
    low = jnp.where(qrow >= first_len, first_len, 0)
    return (kpos <= qrow) & (kpos >= low)


def attend_kernel(len_ref, q_ref, k_ref, v_ref, o_ref, ol_ref, lse_ref, *, tiles):
    first_len = len_ref[0]
    for i, st in tile_variants(tiles):
        q_base = i * TILE
        start = jnp.where(q_base >= first_len, first_len // TILE, 0)

        @pl.when(start == st)
        def _():
            rows = pl.ds(q_base, TILE)
            keys = pl.ds(st * TILE, (i + 1 - st) * TILE)
            ok = allowed_mask(first_len, q_base, st * TILE, (i + 1 - st) * TILE)
            s = dot_tn(k_ref[:, keys], q_ref[:, rows] * jnp.asarray(0.125, BF))
            s = jnp.where(ok, s, -1000000000.0)
            top = jnp.max(s, axis=0, keepdims=True)
            e = jnp.exp(s - top)
            tot = jnp.sum(e, axis=0, keepdims=True)
            soft = (e * (1.0 / tot)).astype(BF)
            o = dot_nn(v_ref[:, keys], soft)
            o_ref[:, rows] = o
            ol_ref[:, rows] = o.astype(BF)
            lse_ref[0, :, rows] = top + jnp.log(tot)


def attend(first_len, qkv, heads):
    group = qkv.shape[1]
    rows = heads * 64
    block = lambda off: pl.BlockSpec((64, group), lambda h, t, off=off: (off + h, 0))
    return call(
        functools.partial(attend_kernel, tiles=group // TILE),
        (first_len,),
        (heads,),
        [(qkv, block(0)), (qkv, block(heads)), (qkv, block(2 * heads))],
        [
            ((rows, group), F32, block(0)),
            ((rows, group), BF, block(0)),
            ((heads, 1, group), F32, pl.BlockSpec((1, 1, group), lambda h, t: (h, 0, 0))),
        ],
        flops=LONG,
    )


def attend_back_kernel(
    len_ref, q_ref, k_ref, v_ref, g_ref, o_ref, lse_ref, out_ref, dk_acc, dv_acc, *, tiles
):
    first_len = len_ref[0]
    dk_acc[...] = jnp.zeros_like(dk_acc)
    dv_acc[...] = jnp.zeros_like(dv_acc)
    for i, st in tile_variants(tiles):
        q_base = i * TILE
        start = jnp.where(q_base >= first_len, first_len // TILE, 0)

        @pl.when(start == st)
        def _():
            rows = pl.ds(q_base, TILE)
            keys = pl.ds(st * TILE, (i + 1 - st) * TILE)
            q = q_ref[:, rows] * jnp.asarray(0.125, BF)
            k = k_ref[:, keys]
            v = v_ref[:, keys]
            g = g_ref[:, rows]
            delta = jnp.sum(g.astype(F32) * o_ref[:, rows], axis=0, keepdims=True)
            ok = allowed_mask(first_len, q_base, st * TILE, (i + 1 - st) * TILE)
            s = dot_tn(k, q)
            soft = jnp.exp(jnp.where(ok, s, -1000000000.0) - lse_ref[0, :, rows])
            dp = dot_tn(v, g)
            ds = (soft * (dp - delta)).astype(BF)
            dv_acc[:, keys] += dot_nt(g, soft.astype(BF))
            dk_acc[:, keys] += dot_nt(q, ds)
            out_ref[0, :, rows] = (dot_nn(k, ds) * 0.125).astype(BF)

    out_ref[1] = dk_acc[...].astype(BF)
    out_ref[2] = dv_acc[...].astype(BF)


def attend_back(first_len, qkv, g, o, lse, heads):
    group = qkv.shape[1]
    rows = heads * 64
    block = lambda off: pl.BlockSpec((64, group), lambda h, t, off=off: (off + h, 0))
    return call(
        functools.partial(attend_back_kernel, tiles=group // TILE),
        (first_len,),
        (heads,),
        [
            (qkv, block(0)),
            (qkv, block(heads)),
            (qkv, block(2 * heads)),
            (g, block(0)),
            (o, block(0)),
            (lse, pl.BlockSpec((1, 1, group), lambda h, t: (h, 0, 0))),
        ],
        [((3, rows, group), BF, pl.BlockSpec((3, 64, group), lambda h, t: (0, h, 0)))],
        [pltpu.VMEM((64, group), F32), pltpu.VMEM((64, group), F32)],
        flops=LONG,
    )[0]


def join_kernel(pos_ref, x_ref, out):
    rows = out.shape[0]
    per = x_ref.shape[1] // BLK
    for j in range(out.shape[1] // BLK):
        at = pl.multiple_of(pos_ref[j] * BLK, BLK)
        chunk = (j // per) * rows
        out[:, pl.ds(at, BLK)] = x_ref[chunk : chunk + rows, (j % per) * BLK : (j % per + 1) * BLK]


def join_blocks(pos, x, count):
    rows, tok = x.shape[0] // count, x.shape[1]
    shape = (rows, count * tok)
    return call(join_kernel, (pos,), (1,), [(x, whole(x))], [(shape, x.dtype, fixed(shape))])[0]


def split_kernel(tab_ref, x_ref, out_ref, *, per):
    rows = x_ref.shape[0]
    store_slots(out_ref, slot_places(tab_ref, rows, per), pl.ds(0, rows), x_ref[...])


def split_call(tab, x, shards):
    width, group = x.shape
    tok = group // shards
    shape = (shards * width, tok)
    return call(
        functools.partial(split_kernel, per=tok // BLK),
        (tab,),
        (group // TILE,),
        [(x, tokens(width))],
        [(shape, BF, fixed(shape))],
    )[0]


def split_sums_kernel(tab_ref, e_ref, xb_ref, out_ref, gain_ref, shift_ref, gain_acc, shift_acc, *, per):
    clear_first(gain_acc, shift_acc)
    rows = e_ref.shape[0]
    places = slot_places(tab_ref, rows, per)

    def finish(at, carry):
        e = e_ref[at, :]
        ex = e * xb_ref[at, :].astype(F32)
        gain_acc[at, :] += ex[:, :BLK] + ex[:, BLK:]
        shift_acc[at, :] += e[:, :BLK] + e[:, BLK:]
        store_slots(out_ref, places, at, e)
        return carry

    sweep(rows, finish, 0)

    @pl.when(pl.program_id(0) == pl.num_programs(0) - 1)
    def _():
        gain_ref[...] = jnp.sum(gain_acc[...], axis=1, keepdims=True)
        shift_ref[...] = jnp.sum(shift_acc[...], axis=1, keepdims=True)


def split_sums_call(tab, e, x, shards):
    width, group = e.shape
    tok = group // shards
    shape = (shards * width, tok)
    return call(
        functools.partial(split_sums_kernel, per=tok // BLK),
        (tab,),
        (group // TILE,),
        [(e, tokens(width)), (x, tokens(width))],
        [(shape, BF, fixed(shape))] + [((width, 1), F32, fixed((width, 1)))] * 2,
        [pltpu.VMEM((width, BLK), F32), pltpu.VMEM((width, BLK), F32)],
    )


def first_back_kernel(
    tab_ref, g_ref, h0_ref, h1_ref, w_ref, ea_ref, gain_ref, shift_ref, gain_acc, shift_acc, e_ref, *, per
):
    clear_first(gain_acc, shift_acc)
    rows = w_ref.shape[0]
    e_ref[...] = dot_nn(w_ref[...], g_ref[...])
    places = slot_places(tab_ref, rows, per)
    loads = [lambda at, ref=ref: ref[at, :].astype(F32) for ref in (h0_ref, h1_ref)]
    stats = [norm_stats(load, rows, BLK) for load in loads]

    def finish(at, carry):
        e = e_ref[at, :]
        store_slots(ea_ref, places, at, e)
        total = jnp.zeros((at.size, BLK), F32)
        for j, (load, (mean, rstd)) in enumerate(zip(loads, stats)):
            total = total + e[:, j * BLK : (j + 1) * BLK] * ((load(at) - mean) * rstd)
        gain_acc[at, :] += total
        shift_acc[at, :] += e[:, :BLK] + e[:, BLK:]
        return carry

    sweep(rows, finish, 0)

    @pl.when(pl.program_id(0) == pl.num_programs(0) - 1)
    def _():
        gain_ref[...] = jnp.sum(gain_acc[...], axis=1, keepdims=True)
        shift_ref[...] = jnp.sum(shift_acc[...], axis=1, keepdims=True)


def first_back_call(tab, g_mixed, hidden_all, w, shards):
    width = w.shape[0]
    inner, group = g_mixed.shape
    tok = group // shards
    per = tok // BLK
    return call(
        functools.partial(first_back_kernel, per=per),
        (tab,),
        (group // TILE,),
        [
            (g_mixed, tokens(inner)),
            (hidden_all, slot_block(width, per, 0)),
            (hidden_all, slot_block(width, per, 1)),
            (w, whole(w)),
        ],
        [
            ((shards * width, tok), BF, fixed((shards * width, tok))),
            ((width, 1), F32, fixed((width, 1))),
            ((width, 1), F32, fixed((width, 1))),
        ],
        [pltpu.VMEM((width, BLK), F32), pltpu.VMEM((width, BLK), F32), pltpu.VMEM((width, TILE), F32)],
        flops=LONG,
    )


def branch_kernel(
    eb_ref, mid_ref, cot_ref, small_ref, w_ref, mg_ref, gb_ref, send_ref, bias_ref, att_ref, *, cuts
):
    rows, tok = mid_ref.shape

    def write(at, value):
        grad = cot_ref[at, :].astype(F32) + value
        mg_ref[at, :] = grad
        low = grad.astype(BF)
        gb_ref[at, :] = low
        bias_ref[at, :] = jnp.sum(low.astype(F32), axis=1, keepdims=True)

    norm_back(
        lambda at: mid_ref[at, :], lambda at: eb_ref[at, :].astype(F32), small_ref, 5, rows, tok, write
    )
    att_ref[...] = dot_nn(w_ref[...], gb_ref[...]).astype(BF)
    send_ref[...] = jnp.zeros_like(send_ref)
    for to, lo, hi in cuts:
        send_ref[to : to + hi - lo, :] = att_ref[lo:hi, :]


def branch_call(e_b_own, middle_own, cot_own, small, w_out, cuts, send_rows):
    width, tok = middle_own.shape
    return call(
        functools.partial(branch_kernel, cuts=cuts),
        (),
        (1,),
        [(x, whole(x)) for x in (e_b_own, middle_own, cot_own, small, w_out)],
        [
            (shape, dtype, fixed(shape))
            for shape, dtype in (
                ((width, tok), F32),
                ((width, tok), BF),
                ((send_rows, tok), BF),
                ((width, 1), F32),
            )
        ],
        [pltpu.VMEM((w_out.shape[0], tok), BF)],
    )


def input_kernel(ea_ref, h_ref, mg_ref, small_ref, out_ref):
    def write(at, value):
        out_ref[at, :] = mg_ref[at, :] + value

    rows, tok = mg_ref.shape
    norm_back(
        lambda at: h_ref[at, :].astype(F32),
        lambda at: ea_ref[at, :].astype(F32),
        small_ref,
        0,
        rows,
        tok,
        write,
    )


def input_call(e_a_own, hidden_own, middle_grad, small):
    shape = middle_grad.shape
    return call(
        input_kernel,
        (),
        (1,),
        [(x, whole(x)) for x in (e_a_own, hidden_own, middle_grad, small)],
        [(shape, F32, fixed(shape))],
    )[0]


def half_of(acc_ref, bit, count):
    return acc_ref[pl.ds(pl.multiple_of(bit * count, 8), count), :].astype(BF)


def grad_kernel(core_ref, a_ref, b_ref, small_ref, keep_ref, *refs):
    sends, acc_ref = refs[:-1], refs[-1]
    rows = a_ref.shape[0]
    count = keep_ref.shape[1]
    extra = acc_ref.shape[0] - rows - SMALL_ROWS
    acc_ref[0:rows, :] = dot_nt(a_ref[...], b_ref[...])
    acc_ref[rows : rows + SMALL_ROWS, :] = small_ref[0]
    acc_ref[rows + SMALL_ROWS :, :] = jnp.zeros((extra, acc_ref.shape[1]), F32)
    keep_ref[0] = half_of(acc_ref, core_ref[0], count)
    for n, send_ref in enumerate(sends):

        @pl.when(pl.program_id(0) == n)
        def _(send_ref=send_ref):
            send_ref[...] = half_of(acc_ref, 1 - core_ref[0], count)


def grad_call(core, a, b, small, half, flops):
    lead, _, cols = small.shape
    rows, group = a.shape[0] // lead, a.shape[1]
    keep = ((lead, half, cols), BF, pl.BlockSpec((1, half, cols), lambda i, *_: (i, 0, 0)))
    outs = call(
        grad_kernel,
        (core,),
        (lead,),
        [
            (a, pl.BlockSpec((rows, group), lambda i, *_: (i, 0))),
            (b, whole(b)),
            (small, pl.BlockSpec((1, SMALL_ROWS, cols), lambda i, *_: (i, 0, 0))),
        ],
        [keep] + [((half, cols), BF, fixed((half, cols)))] * lead,
        [pltpu.VMEM((2 * half, cols), F32)],
        flops,
    )
    return outs[0], outs[1:]


def first_step_kernel(bit_ref, *refs, leads):
    ins, (keep_ref, send_ref, acc_ref) = refs[:-3], refs[-3:]
    count = keep_ref.shape[1]
    first = at = 0
    for lead in leads:
        for n in range(lead):

            @pl.when(pl.program_id(0) == first + n)
            def _(x_ref=ins[at], y_ref=ins[at + 1 + n]):
                acc_ref[...] = x_ref[0].astype(F32) + y_ref[...].astype(F32)

        first += lead
        at += 1 + lead
    keep_ref[0] = half_of(acc_ref, bit_ref[0], count)
    send_ref[0] = half_of(acc_ref, 1 - bit_ref[0], count)


def first_step_call(bit, sums):
    _, count, cols = sums[0][0].shape
    leads = [x.shape[0] for x, _ in sums]
    total = sum(leads)
    ins = []
    first = 0
    for (x, pieces), lead in zip(sums, leads):
        at = lambda i, *_, first=first, lead=lead: (jnp.clip(i - first, 0, lead - 1), 0, 0)
        ins.append((x, pl.BlockSpec((1, count, cols), at)))
        ins += [(y, whole(y)) for y in pieces]
        first += lead
    part = ((total, count // 2, cols), BF, pl.BlockSpec((1, count // 2, cols), lambda i, *_: (i, 0, 0)))
    return call(
        functools.partial(first_step_kernel, leads=leads),
        (bit,),
        (total,),
        ins,
        [part, part],
        [pltpu.VMEM((count, cols), F32)],
    )


def wide_step_kernel(bit_ref, *refs, lead, wide):
    ins, (keep_ref, send_ref, acc_ref) = refs[:-3], refs[-3:]
    count = keep_ref.shape[1]
    end = 0
    for x_at, lo, hi in wide:
        if lo > end:
            acc_ref[:, end:lo] = jnp.zeros((acc_ref.shape[0], lo - end), F32)
        end = hi
        for n in range(lead):

            @pl.when(pl.program_id(0) == n)
            def _(x_ref=ins[x_at], y_ref=ins[x_at + 1 + n], lo=lo, hi=hi):
                acc_ref[:, lo:hi] = x_ref[0].astype(F32) + y_ref[...].astype(F32)

    keep_ref[0] = half_of(acc_ref, bit_ref[0], count)
    send_ref[0] = half_of(acc_ref, 1 - bit_ref[0], count)


def wide_step_call(bit, sums, offsets, cols):
    lead, count, _ = sums[0][0].shape
    ins, wide = [], []
    for (x, pieces), lo in zip(sums, offsets):
        wide.append((len(ins), lo, lo + x.shape[2]))
        ins.append((x, pl.BlockSpec((1, count, x.shape[2]), lambda i, *_: (i, 0, 0))))
        ins += [(y, whole(y)) for y in pieces]
    part = ((lead, count // 2, cols), BF, pl.BlockSpec((1, count // 2, cols), lambda i, *_: (i, 0, 0)))
    return call(
        functools.partial(wide_step_kernel, lead=lead, wide=wide),
        (bit,),
        (lead,),
        ins,
        [part, part],
        [pltpu.VMEM((count, cols), F32)],
        flops=SHORT,
    )


def step_kernel(bit_ref, x_ref, y_ref, keep_ref, send_ref, acc_ref):
    count = keep_ref.shape[1]
    acc_ref[...] = x_ref[0].astype(F32) + y_ref[0].astype(F32)
    keep_ref[0] = half_of(acc_ref, bit_ref[0], count)
    send_ref[0] = half_of(acc_ref, 1 - bit_ref[0], count)


def step_call(bit, x, y, flops):
    lead, count, cols = x.shape
    block = pl.BlockSpec((1, count, cols), lambda i, *_: (i, 0, 0))
    part = ((lead, count // 2, cols), BF, pl.BlockSpec((1, count // 2, cols), lambda i, *_: (i, 0, 0)))
    return call(
        step_kernel, (bit,), (lead,), [(x, block), (y, block)], [part, part], [pltpu.VMEM((count, cols), F32)], flops
    )


def place_kernel(at_ref, mine_ref, theirs_ref, *refs, spans):
    outs, acc_ref = refs[:-1], refs[-1]
    pieces, _, count, _ = mine_ref.shape
    rows = outs[0].shape[1]
    for n in range(2 * pieces):
        at = pl.multiple_of(at_ref[n], 8)
        acc_ref[pl.ds(at, count), :] = (theirs_ref if n >= pieces else mine_ref)[n % pieces, 0].astype(F32)
    for n, (lo, hi) in enumerate(spans):
        outs[2 * n][0] = acc_ref[0:rows, lo:hi]
        outs[2 * n + 1][0] = acc_ref[rows : rows + SMALL_ROWS, lo:hi]


def place_call(places, mine, theirs, rows, spans):
    pieces, lead, count, cols = mine.shape
    cut = 1280 if cols % 1280 == 0 and len(spans) == 1 else cols
    block = pl.BlockSpec((pieces, 1, count, cut), lambda i, j, *_: (0, i, 0, j))
    outs = []
    for lo, hi in spans:
        lanes = min(hi - lo, cut)
        for height in (rows, SMALL_ROWS):
            spec = pl.BlockSpec((1, height, lanes), lambda i, j, *_: (i, 0, j))
            outs.append(((lead, height, hi - lo), F32, spec))
    inner = [(0, cut)] if len(spans) == 1 else spans
    return call(
        functools.partial(place_kernel, spans=inner),
        (places,),
        (lead, cols // cut),
        [(mine, block), (theirs, block)],
        outs,
        [pltpu.VMEM((2 * pieces * count, cut), F32)],
        flops=SHORT,
    )


ROOT = 0.7978845608028654
CUBE = 0.044715


def gelu(u):
    return 0.5 * u * (1.0 + jnp.tanh(ROOT * (u + CUBE * u * u * u)))


def gelu_slope(u):
    bend = jnp.tanh(ROOT * (u + CUBE * u * u * u))
    return 0.5 * (1.0 + bend) + 0.5 * u * (1.0 - bend * bend) * (ROOT * (1.0 + 3.0 * CUBE * u * u))


def token_sum(values_in):
    return jnp.sum(values_in.astype(F32), axis=1)


def after(x, *first):
    return lax.optimization_barrier((x,) + first)[0]


def together(*values):
    return lax.optimization_barrier(values)


def per_device(
    chips,
    shards,
    hidden_in,
    cotangent,
    slot_index,
    seq_lengths,
    attn_gain,
    attn_shift,
    attn_weight,
    query_bias,
    value_bias,
    out_weight,
    out_bias,
    mlp_gain,
    mlp_shift,
    up_weight,
    up_bias,
    down_weight,
    down_bias,
):
    tok, width = hidden_in.shape
    group = slot_index.shape[0]
    head = width // H
    rows = width // shards
    ff_own = down_weight.shape[0]
    counts, starts, windows, win = head_plan(shards)
    wc = win * head
    reps = 2 * chips
    piece = -(-(rows + SMALL_ROWS) // (8 * reps)) * 8
    half = chips * piece
    me = lax.axis_index("shard")
    chip = lax.axis_index("chip")
    core = lax.axis_index("core")
    blocks = group // BLK
    own_blocks = tok // BLK
    spans = []
    for s in range(shards):
        lo = (starts[s] - windows[s]) * head
        spans.append((s * wc + lo, s * wc + lo + counts[s] * head))

    def to_next(x, t):
        return lax.ppermute(x, "shard", [(i, (i + t) % shards) for i in range(shards)])

    def other_core(x):
        return lax.ppermute(x, "core", [(0, 1), (1, 0)])

    def pick(x, at):
        return lax.dynamic_index_in_dim(x, at, 0, keepdims=False)

    def turn(j):
        return lax.rem(j + 2 * shards, shards)

    def exchange(send):
        got = [pick(send, me)]
        for t in range(1, shards):
            got.append(to_next(pick(send, turn(me + t)), t))
        got = jnp.stack(got)
        return jnp.stack([pick(got, turn(me - j)) for j in range(shards)])

    def over_shard(x):
        return lax.all_gather(x, "shard", axis=0, tiled=True)

    def window(x, s):
        return x[..., windows[s] * head : windows[s] * head + wc]

    def scalar(x):
        return jnp.reshape(x, (1,)).astype(jnp.int32)

    square = chips == 4
    bits = (chip // 2, chip % 2)
    first_bit = jnp.where(core == 0, bits[1], bits[0])
    second_bit = jnp.where(core == 0, bits[0], bits[1])
    slot = 2 * first_bit + second_bit if square else chip
    other_slot = 2 * second_bit + first_bit

    def flip(x, step):
        pairs = []
        for q in range(chips):
            for c in range(2):
                partner = q ^ 1 if (c + step) % 2 == 0 else q ^ 2
                pairs.append((2 * q + c, 2 * partner + c))
        return lax.ppermute(x, ("chip", "core"), pairs)

    def add_low(x, y):
        return (x.astype(F32) + y.astype(F32)).astype(BF)

    def sum_start(a, b, small, *first, flops=1024):
        keep, sends = grad_call(after(scalar(core), *first), a, b, small, half, flops)
        return keep, [other_core(x) for x in sends]

    def chip_sum(state):
        x = add_low(state[0], jnp.stack(state[1]))
        x = jnp.swapaxes(x.reshape(x.shape[0], chips, piece, x.shape[2]), 0, 1)
        return lax.psum_scatter(x, "chip", scatter_dimension=0, tiled=False)

    def sum_second(state, *first, flops=1024):
        if not square:
            return state
        keep, send = step_call(after(scalar(second_bit), *first), *state, flops)
        return keep, flip(send, 1)

    def sum_last(state):
        return add_low(*state) if square else state[0]

    def spread_near(x):
        return jnp.stack([x, flip(x, 1)]) if square else x

    def spread_far(x):
        if not square:
            return lax.all_gather(x, "chip", axis=0, tiled=False)
        return jnp.concatenate([x, flip(x, 0)], axis=0)

    def spread_last(mine, spans, *first):
        places = []
        for c, at in ((core, slot), (1 - core, other_slot)):
            for j in range(chips):
                places.append(c * half + ((at ^ j) if square else j) * piece)
        places = after(jnp.stack(places).astype(jnp.int32), *first)
        return place_call(places, mine, other_core(mine), rows, spans)

    def in_order(bit, x, y):
        return jnp.concatenate([jnp.where(bit == 0, x, y), jnp.where(bit == 0, y, x)], axis=1)

    def my_piece(x):
        x = jnp.pad(x, ((0, 2 * half - x.shape[0]), (0, 0)))
        return lax.dynamic_slice_in_dim(x, core * half + slot * piece, piece, 0)

    def weight_near(x):
        return in_order(second_bit, x, flip(x, 1)) if square else x

    def weight_far(x, *first):
        if not square:
            x = jnp.swapaxes(lax.all_gather(x, "chip", axis=0, tiled=False), 0, 1)
            return x.reshape(x.shape[0], -1, x.shape[-1])
        return in_order(first_bit, after(x, *first) if first else x, flip(x, 0))

    def weight_rows(x):
        x = in_order(core, x, other_core(x))
        return x[:, :rows].reshape(shards * rows, x.shape[-1])

    def small_block(vectors, cols):
        x = jnp.stack(vectors).reshape(len(vectors), shards, rows)
        pad = ((0, 0), (0, SMALL_ROWS - len(vectors)), (0, cols - rows))
        return jnp.pad(jnp.swapaxes(x, 0, 1), pad)

    def with_sum(x, got):
        total = jnp.sum(got[:, :, :rows].astype(F32), axis=0).astype(BF)
        total = jnp.pad(total, ((0, 0), (0, x.shape[1] - rows)))
        row = core * half + slot * piece + lax.broadcasted_iota(jnp.int32, (piece, 1), 0)
        return jnp.where(row >= rows, total, x)[None]

    pos = (slot_index.reshape(blocks, BLK)[:, 0] // BLK).astype(jnp.int32)
    ids = jnp.arange(blocks, dtype=jnp.int32)
    tab = jnp.sum(jnp.where(pos[None, :] == ids[:, None], ids[None, :], 0), axis=1).astype(jnp.int32)
    first_len = seq_lengths[0, :1]

    hidden_own = hidden_in.T
    cot_own = cotangent.T
    small = jnp.stack(
        [attn_gain, attn_shift, query_bias, value_bias, out_bias, mlp_gain, mlp_shift, down_bias]
    )
    small = jnp.pad(small, ((0, 0), (0, 3 * wc - rows)))
    attn_piece = my_piece(attn_weight)
    parts = []
    for s in range(shards):
        cut = [window(attn_piece[:, j * width : (j + 1) * width], s) for j in range(3)]
        parts.append(jnp.concatenate([jnp.concatenate(cut, axis=1), small], axis=0))
    attn_got = exchange(jnp.stack(parts))
    small = jnp.swapaxes(attn_got[:, piece:, :rows], 0, 1).reshape(SMALL_ROWS, width)
    small = small.astype(F32).T
    hidden_all = over_shard(hidden_own)
    attn_near = after(weight_near(attn_got[:, :piece]), hidden_all)
    attn_far = weight_far(attn_near)
    normed_a, hidden = first_norm_call(tab, hidden_all, small, shards)
    w_qkv = weight_rows(after(attn_far, normed_a))
    out_piece = after(my_piece(out_weight), hidden_all)
    out_got = exchange(jnp.stack([out_piece] * shards))
    out_near = weight_near(after(out_got, attn_far))
    up_piece = after(my_piece(up_weight), out_got)
    up_got = exchange(jnp.stack([up_piece[:, s * ff_own : (s + 1) * ff_own] for s in range(shards)]))

    bias_rows = jnp.stack(
        [
            jnp.concatenate(
                [window(small[:, 2], s), jnp.zeros((wc,), F32), window(small[:, 3], s)]
            )
            for s in range(shards)
        ]
    )
    bias_qkv = after(pick(bias_rows, me)[:, None], up_got)
    qkv = (dot_tn(w_qkv, normed_a) + bias_qkv).astype(BF)
    w_out = weight_rows(weight_far(out_near, qkv))
    attended, attended_low, lse = attend(after(first_len, w_out), qkv, win)
    att_all = over_shard(attended_low)
    up_near = weight_near(after(up_got, attended_low))
    w_up = weight_rows(weight_far(after(up_near, att_all)))

    cot_all = over_shard(after(cot_own, att_all))
    att_full = jnp.concatenate([att_all[lo:hi] for lo, hi in spans], axis=0)
    middle = hidden.astype(F32) + dot_tn(w_out, att_full) + small[:, 4:5]
    average = jnp.mean(middle, axis=0, keepdims=True)
    centred = middle - average
    variance = jnp.mean(centred * centred, axis=0, keepdims=True)
    x_b = centred * lax.rsqrt(variance + EPSILON)
    normed_b = (x_b * small[:, 5:6] + small[:, 6:7]).astype(BF)
    x_b = x_b.astype(BF)

    def own_tokens(x):
        parts = [
            lax.dynamic_slice_in_dim(x, pos[me * own_blocks + j] * BLK, BLK, 1)
            for j in range(own_blocks)
        ]
        return jnp.concatenate(parts, axis=1)

    pre = dot_tn(w_up, normed_b) + up_bias.astype(F32)[:, None]
    act = gelu(pre).astype(BF)
    ffn_part = split_call(tab, dot_tn(down_weight, act).astype(BF), shards)
    ffn_chunks = ffn_part.reshape(shards, width, tok)

    def ffn_send(t, part, *first):
        return to_next(after(pick(ffn_chunks, turn(me + t))[part], *first), t)

    ffn_own = pick(ffn_chunks, me).astype(F32)
    ffn_near = ffn_send(1, slice(None))
    cot = join_blocks(after(pos, ffn_part), cot_all, shards)
    g_pre = (dot_nn(down_weight, cot) * gelu_slope(pre)).astype(BF)
    e_b = dot_nn(w_up, g_pre) + after(jnp.zeros((), F32), ffn_near)
    e_b, g_mlp_gain, g_mlp_shift = split_sums_call(tab, e_b, x_b, shards)
    ffn_own = ffn_own + ffn_near.astype(F32)
    middle_own = own_tokens(after(middle, e_b))
    g_up_bias = token_sum(after(g_pre, e_b))[:, None]

    def token_scatter(x):
        return lax.psum_scatter(x, "shard", scatter_dimension=0, tiled=True)

    e_b_own = token_scatter(e_b)
    lead = ff_own // rows
    small_down = jnp.pad(
        g_up_bias[:, 0][None, None], ((0, lead - 1), (0, SMALL_ROWS - 1), (0, width - ff_own))
    )
    down_sum = sum_start(act, cot, small_down, e_b)
    small_up = small_block([g_mlp_gain[:, 0], g_mlp_shift[:, 0], token_sum(cot_own)], ff_own)
    up_sum = sum_start(normed_b, g_pre, small_up, down_sum[0])
    merged = square and ff_own == width
    if merged:
        keep, send = first_step_call(scalar(first_bit), [down_sum, up_sum])
        ffn_sum = (keep, flip(send, 0))
    else:
        ffn_sum = (chip_sum(down_sum), chip_sum(up_sum))
    e_b_own, keep = together(e_b_own, ffn_sum[0])
    ffn_sum = (keep,) + ffn_sum[1:]

    cuts = [(lo, lo - s * wc + windows[s] * head, hi - s * wc + windows[s] * head) for s, (lo, hi) in enumerate(spans)]
    middle_grad, g_branch, sends, g_out_bias = branch_call(
        e_b_own, middle_own, cot_own, small, w_out, cuts, shards * wc
    )
    g_att = exchange(sends.reshape(shards, wc, tok)).reshape(shards * wc, tok)
    att_own = own_tokens(att_full)
    if merged:
        ffn_sum = sum_second(ffn_sum, sends)
    out_sum = sum_start(att_own, g_branch, small_block([g_out_bias[:, 0]], width), ffn_sum[0])
    keep_out = out_sum[0]
    ffn_back = ffn_send(shards - 1, slice(None), g_att)
    g_att = join_blocks(pos, g_att, shards)
    g_mixed = attend_back(first_len, qkv, g_att, attended, lse, win)
    g_mixed_rows = g_mixed.reshape(3 * wc, group)

    e_a, g_attn_gain, g_attn_shift = first_back_call(
        after(tab, keep_out, ffn_back), g_mixed_rows, hidden_all, w_qkv, shards
    )
    e_a_own = token_scatter(e_a)
    ffn_own = ffn_own + ffn_back.astype(F32)
    if merged:
        ffn_last = after(sum_last(ffn_sum), e_a)
        down_own, up_own = ffn_last[:lead], ffn_last[lead:]
    else:
        down_own, up_own = ffn_sum
    up_got = exchange(up_own)
    down_near = spread_near(down_own)
    up_row = with_sum(jnp.concatenate([up_got[s] for s in range(shards)], axis=-1), up_got)
    up_near = spread_near(up_row)
    cut = width // 2
    ffn_top = [ffn_send(t, slice(0, cut), e_a_own) for t in range(2, shards - 1)]
    ffn_low = [ffn_send(t, slice(cut, None), *ffn_top) for t in range(2, shards - 1)]
    for top, low in zip(ffn_top, ffn_low):
        ffn_own = ffn_own + jnp.concatenate([top, low], axis=0).astype(F32)

    def place(x):
        outs = [
            jnp.pad(x, (windows[s] * head, width - windows[s] * head - wc)) for s in range(shards)
        ]
        return pick(jnp.stack(outs), me)

    sums = jnp.sum(g_mixed.astype(F32), axis=2)
    small_mix = small_block(
        [g_attn_gain[:, 0], g_attn_shift[:, 0], place(sums[0]), place(sums[2])], 3 * wc
    )
    mix_sum = sum_start(normed_a, g_mixed_rows, small_mix)
    down_mine = spread_far(down_near)

    skip = -(-width // BLK) * BLK
    if square:
        keep, send = wide_step_call(
            after(scalar(first_bit), down_near), [(keep_out, out_sum[1]), mix_sum], (0, skip), skip + 3 * wc
        )
        g_down_full, down_small = spread_last(down_mine, [(0, width)], keep)
        wide_sum = sum_second((keep, flip(send, 0)), g_down_full, up_near, *ffn_top, flops=SHORT)
        wide_own = sum_last(wide_sum)
    else:
        gap = jnp.zeros((shards, piece, skip - width), BF)
        wide_own = jnp.concatenate([chip_sum((keep_out, out_sum[1])), gap, chip_sum(mix_sum)], axis=-1)
        g_down_full, down_small = spread_last(down_mine, [(0, width)])
    wide_own = after(wide_own, e_a_own, *ffn_low)
    wide_got = exchange(wide_own)
    up_mine = spread_far(after(up_near, wide_own))
    g_up_full, up_small = spread_last(up_mine, [(0, shards * ff_own)])
    columns = []
    for j in range(3):
        for s in range(shards):
            lo, hi = skip + j * wc + spans[s][0] - s * wc, skip + j * wc + spans[s][1] - s * wc
            columns.append(wide_got[s, :, lo:hi])
    mix_row = with_sum(jnp.concatenate(columns, axis=-1), wide_got[:, :, skip:])
    out_row = jnp.sum(wide_got[:, :, :skip].astype(F32), axis=0).astype(BF)
    wide_row = jnp.concatenate([out_row[None], mix_row], axis=-1)
    wide_near = after(spread_near(wide_row), g_up_full)
    g_out_full, out_small, g_mix_full, mix_small = spread_last(
        spread_far(wide_near), [(0, width), (skip, skip + 3 * width)]
    )

    block_out = (middle_own + ffn_own + small[:, 7:8]).astype(BF).T
    input_grad = input_call(e_a_own, hidden_own, middle_grad, small).T

    return (
        block_out,
        input_grad,
        mix_small[0, 0, :rows],
        mix_small[0, 1, :rows],
        g_mix_full[0],
        mix_small[0, 2, :rows],
        mix_small[0, 3, :rows],
        g_out_full[0],
        out_small[0, 0, :rows],
        up_small[0, 0, :rows],
        up_small[0, 1, :rows],
        g_up_full[0],
        down_small[0, 0, :ff_own],
        g_down_full.reshape(ff_own, width),
        up_small[0, 2, :rows],
    )


def solution(mesh):
    reps, shards = mesh.shape["rep"], mesh.shape["shard"]
    fine = Mesh(mesh.devices.reshape(reps // 2, 2, shards), ("chip", "core", "shard"))
    rep = ("chip", "core")
    both = ("chip", "core", "shard")
    return jax.shard_map(
        functools.partial(per_device, reps // 2, shards),
        mesh=fine,
        in_specs=(
            P(both, None),
            P(both, None),
            P(rep),
            P(rep, None),
            P("shard"),
            P("shard"),
            P("shard", None),
            P("shard"),
            P("shard"),
            P("shard", None),
            P("shard"),
            P("shard"),
            P("shard"),
            P("shard", None),
            P("shard"),
            P("shard", None),
            P("shard"),
        ),
        out_specs=(
            P(both, None),
            P(both, None),
            P("shard"),
            P("shard"),
            P("shard", None),
            P("shard"),
            P("shard"),
            P("shard", None),
            P("shard"),
            P("shard"),
            P("shard"),
            P("shard", None),
            P("shard"),
            P("shard", None),
            P("shard"),
        ),
        check_vma=False,
    )
```

```python
import functools

import jax
import jax.numpy as jnp
from jax import lax
from jax.experimental import pallas as pl
from jax.experimental.pallas import tpu as pltpu
from jax.sharding import Mesh
from jax.sharding import PartitionSpec as P

H = 25
BLK = 128
TILE = 256
EPSILON = 1e-05
BF = jnp.bfloat16
F32 = jnp.float32
VMEM_LIMIT = 56 * 1024 * 1024
SMALL_ROWS = 8


def dot_nt(a, b):
    return lax.dot_general(a, b, (((1,), (1,)), ((), ())), preferred_element_type=F32)


def dot_tn(a, b):
    return lax.dot_general(a, b, (((0,), (0,)), ((), ())), preferred_element_type=F32)


def dot_nn(a, b):
    return lax.dot_general(a, b, (((1,), (0,)), ((), ())), preferred_element_type=F32)


def head_plan(shards):
    base, extra = H // shards, H % shards
    counts = [base + (1 if s < extra else 0) for s in range(shards)]
    starts = [sum(counts[:s]) for s in range(shards)]
    width = max(counts)
    windows = [min(st, H - width) for st in starts]
    return counts, starts, windows, width


LONG = 20_000_000_000
SHORT = 10_000_000_000


def call(kernel, scalars, grid, ins, outs, scratch=(), flops=1024):
    return pl.pallas_call(
        kernel,
        out_shape=[jax.ShapeDtypeStruct(shape, dtype) for shape, dtype, _ in outs],
        grid_spec=pltpu.PrefetchScalarGridSpec(
            num_scalar_prefetch=len(scalars),
            grid=grid,
            in_specs=[spec for _, spec in ins],
            out_specs=[spec for _, _, spec in outs],
            scratch_shapes=list(scratch),
        ),
        compiler_params=pltpu.CompilerParams(vmem_limit_bytes=VMEM_LIMIT),
        cost_estimate=pl.CostEstimate(flops=flops, bytes_accessed=1024, transcendentals=0),
    )(*scalars, *[array for array, _ in ins])


def whole(array):
    zeros = (0,) * array.ndim
    return pl.BlockSpec(array.shape, lambda *_: zeros, pipeline_mode=pl.Buffered(1))


def fixed(shape):
    zeros = (0,) * len(shape)
    return pl.BlockSpec(shape, lambda *_: zeros)


def tokens(rows):
    return pl.BlockSpec((rows, TILE), lambda i, *_: (0, i))


def slot_block(rows, per, which):
    return pl.BlockSpec(
        (rows, BLK), lambda i, tab, *_: (tab[2 * i + which] // per, lax.rem(tab[2 * i + which], per))
    )


STEP = 80


def sweep(rows, body, carry, step=STEP):
    while rows % step:
        step -= 16
    for at in range(0, rows, step):
        carry = body(pl.ds(at, step), carry)
    return carry


def chunk(rows, lanes):
    step = STEP
    while rows % step:
        step -= 16
    return jnp.zeros((step, lanes), F32)


def column_mean(acc, rows):
    return jnp.sum(acc, axis=0, keepdims=True) * (1.0 / rows)


def norm_stats(load, rows, lanes):
    zero = chunk(rows, lanes)
    mean = column_mean(sweep(rows, lambda at, acc: acc + load(at), zero), rows)

    def spread(at, acc):
        centred = load(at) - mean
        return acc + centred * centred

    return mean, lax.rsqrt(column_mean(sweep(rows, spread, zero), rows) + EPSILON)


def norm_back(load, load_e, gain_ref, col, rows, lanes, write):
    mean, rstd = norm_stats(load, rows, lanes)
    zero = chunk(rows, lanes)

    def both(at):
        return (load(at) - mean) * rstd, load_e(at) * gain_ref[at, col : col + 1]

    def sums(at, carry):
        x, c = both(at)
        return carry[0] + c, carry[1] + c * x

    mean_c, mean_cx = sweep(rows, sums, (zero, zero))
    mean_c, mean_cx = column_mean(mean_c, rows), column_mean(mean_cx, rows)

    def last(at, carry):
        x, c = both(at)
        write(at, rstd * (c - mean_c - x * mean_cx))
        return carry

    sweep(rows, last, 0)


def slot_places(tab_ref, rows, per):
    places = []
    for which in range(2):
        place = tab_ref[2 * pl.program_id(0) + which]
        row = pl.multiple_of((place // per) * rows, 16)
        places.append((row, pl.multiple_of(lax.rem(place, per) * BLK, BLK)))
    return places


def store_slots(out_ref, places, at, value):
    for which, (row, lane) in enumerate(places):
        rows = pl.ds(pl.multiple_of(row + at.start, 16), at.size)
        out_ref[rows, pl.ds(lane, BLK)] = value[:, which * BLK : (which + 1) * BLK].astype(out_ref.dtype)


def clear_first(*refs):
    @pl.when(pl.program_id(0) == 0)
    def _():
        for ref in refs:
            ref[...] = jnp.zeros_like(ref)


def first_norm_kernel(tab_ref, h0_ref, h1_ref, small_ref, na_ref, pack_ref):
    rows = na_ref.shape[0]
    for j, ref in enumerate((h0_ref, h1_ref)):
        load = lambda at, ref=ref: ref[at, :].astype(F32)
        mean, rstd = norm_stats(load, rows, BLK)

        def write(at, carry, load=load, mean=mean, rstd=rstd, j=j):
            x = (load(at) - mean) * rstd
            na_ref[at, j * BLK : (j + 1) * BLK] = (x * small_ref[at, 0:1] + small_ref[at, 1:2]).astype(BF)
            return carry

        pack_ref[:, j * BLK : (j + 1) * BLK] = ref[...]

        sweep(rows, write, 0)


def first_norm_call(tab, hidden_all, small, shards):
    width, tok = small.shape[0], hidden_all.shape[1]
    group = tok * shards
    per = tok // BLK
    return call(
        first_norm_kernel,
        (tab,),
        (group // TILE,),
        [
            (hidden_all, slot_block(width, per, 0)),
            (hidden_all, slot_block(width, per, 1)),
            (small, whole(small)),
        ],
        [((width, group), BF, tokens(width))] * 2,
        flops=LONG,
    )


def tile_variants(tiles):
    return [(i, st) for i in range(tiles) for st in range(i + 1)]


def allowed_mask(first_len, q_base, k_base, k_rows):
    kpos = k_base + lax.broadcasted_iota(jnp.int32, (k_rows, TILE), 0)
    qrow = q_base + lax.broadcasted_iota(jnp.int32, (1, TILE), 1)
    low = jnp.where(qrow >= first_len, first_len, 0)
    return (kpos <= qrow) & (kpos >= low)


def attend_kernel(len_ref, q_ref, k_ref, v_ref, o_ref, ol_ref, lse_ref, *, tiles):
    first_len = len_ref[0]
    for i, st in tile_variants(tiles):
        q_base = i * TILE
        start = jnp.where(q_base >= first_len, first_len // TILE, 0)

        @pl.when(start == st)
        def _():
            rows = pl.ds(q_base, TILE)
            keys = pl.ds(st * TILE, (i + 1 - st) * TILE)
            ok = allowed_mask(first_len, q_base, st * TILE, (i + 1 - st) * TILE)
            s = dot_tn(k_ref[:, keys], q_ref[:, rows] * jnp.asarray(0.125, BF))
            s = jnp.where(ok, s, -1000000000.0)
            top = jnp.max(s, axis=0, keepdims=True)
            e = jnp.exp(s - top)
            tot = jnp.sum(e, axis=0, keepdims=True)
            soft = (e * (1.0 / tot)).astype(BF)
            o = dot_nn(v_ref[:, keys], soft)
            o_ref[:, rows] = o
            ol_ref[:, rows] = o.astype(BF)
            lse_ref[0, :, rows] = top + jnp.log(tot)


def attend(first_len, qkv, heads):
    group = qkv.shape[1]
    rows = heads * 64
    block = lambda off: pl.BlockSpec((64, group), lambda h, t, off=off: (off + h, 0))
    return call(
        functools.partial(attend_kernel, tiles=group // TILE),
        (first_len,),
        (heads,),
        [(qkv, block(0)), (qkv, block(heads)), (qkv, block(2 * heads))],
        [
            ((rows, group), F32, block(0)),
            ((rows, group), BF, block(0)),
            ((heads, 1, group), F32, pl.BlockSpec((1, 1, group), lambda h, t: (h, 0, 0))),
        ],
        flops=LONG,
    )


def attend_back_kernel(
    len_ref, q_ref, k_ref, v_ref, g_ref, o_ref, lse_ref, out_ref, dk_acc, dv_acc, *, tiles
):
    first_len = len_ref[0]
    dk_acc[...] = jnp.zeros_like(dk_acc)
    dv_acc[...] = jnp.zeros_like(dv_acc)
    for i, st in tile_variants(tiles):
        q_base = i * TILE
        start = jnp.where(q_base >= first_len, first_len // TILE, 0)

        @pl.when(start == st)
        def _():
            rows = pl.ds(q_base, TILE)
            keys = pl.ds(st * TILE, (i + 1 - st) * TILE)
            q = q_ref[:, rows] * jnp.asarray(0.125, BF)
            k = k_ref[:, keys]
            v = v_ref[:, keys]
            g = g_ref[:, rows]
            delta = jnp.sum(g.astype(F32) * o_ref[:, rows], axis=0, keepdims=True)
            ok = allowed_mask(first_len, q_base, st * TILE, (i + 1 - st) * TILE)
            s = dot_tn(k, q)
            soft = jnp.exp(jnp.where(ok, s, -1000000000.0) - lse_ref[0, :, rows])
            dp = dot_tn(v, g)
            ds = (soft * (dp - delta)).astype(BF)
            dv_acc[:, keys] += dot_nt(g, soft.astype(BF))
            dk_acc[:, keys] += dot_nt(q, ds)
            out_ref[0, :, rows] = (dot_nn(k, ds) * 0.125).astype(BF)

    out_ref[1] = dk_acc[...].astype(BF)
    out_ref[2] = dv_acc[...].astype(BF)


def attend_back(first_len, qkv, g, o, lse, heads):
    group = qkv.shape[1]
    rows = heads * 64
    block = lambda off: pl.BlockSpec((64, group), lambda h, t, off=off: (off + h, 0))
    return call(
        functools.partial(attend_back_kernel, tiles=group // TILE),
        (first_len,),
        (heads,),
        [
            (qkv, block(0)),
            (qkv, block(heads)),
            (qkv, block(2 * heads)),
            (g, block(0)),
            (o, block(0)),
            (lse, pl.BlockSpec((1, 1, group), lambda h, t: (h, 0, 0))),
        ],
        [((3, rows, group), BF, pl.BlockSpec((3, 64, group), lambda h, t: (0, h, 0)))],
        [pltpu.VMEM((64, group), F32), pltpu.VMEM((64, group), F32)],
        flops=LONG,
    )[0]


def join_kernel(pos_ref, x_ref, out):
    rows = out.shape[0]
    per = x_ref.shape[1] // BLK
    for j in range(out.shape[1] // BLK):
        at = pl.multiple_of(pos_ref[j] * BLK, BLK)
        chunk = (j // per) * rows
        out[:, pl.ds(at, BLK)] = x_ref[chunk : chunk + rows, (j % per) * BLK : (j % per + 1) * BLK]


def join_blocks(pos, x, count):
    rows, tok = x.shape[0] // count, x.shape[1]
    shape = (rows, count * tok)
    return call(join_kernel, (pos,), (1,), [(x, whole(x))], [(shape, x.dtype, fixed(shape))])[0]


def split_kernel(tab_ref, x_ref, out_ref, *, per):
    rows = x_ref.shape[0]
    store_slots(out_ref, slot_places(tab_ref, rows, per), pl.ds(0, rows), x_ref[...])


def split_call(tab, x, shards):
    width, group = x.shape
    tok = group // shards
    shape = (shards * width, tok)
    return call(
        functools.partial(split_kernel, per=tok // BLK),
        (tab,),
        (group // TILE,),
        [(x, tokens(width))],
        [(shape, BF, fixed(shape))],
    )[0]


def split_sums_kernel(tab_ref, e_ref, xb_ref, out_ref, gain_ref, shift_ref, gain_acc, shift_acc, *, per):
    clear_first(gain_acc, shift_acc)
    rows = e_ref.shape[0]
    places = slot_places(tab_ref, rows, per)

    def finish(at, carry):
        e = e_ref[at, :]
        ex = e * xb_ref[at, :].astype(F32)
        gain_acc[at, :] += ex[:, :BLK] + ex[:, BLK:]
        shift_acc[at, :] += e[:, :BLK] + e[:, BLK:]
        store_slots(out_ref, places, at, e)
        return carry

    sweep(rows, finish, 0)

    @pl.when(pl.program_id(0) == pl.num_programs(0) - 1)
    def _():
        gain_ref[...] = jnp.sum(gain_acc[...], axis=1, keepdims=True)
        shift_ref[...] = jnp.sum(shift_acc[...], axis=1, keepdims=True)


def split_sums_call(tab, e, x, shards):
    width, group = e.shape
    tok = group // shards
    shape = (shards * width, tok)
    return call(
        functools.partial(split_sums_kernel, per=tok // BLK),
        (tab,),
        (group // TILE,),
        [(e, tokens(width)), (x, tokens(width))],
        [(shape, BF, fixed(shape))] + [((width, 1), F32, fixed((width, 1)))] * 2,
        [pltpu.VMEM((width, BLK), F32), pltpu.VMEM((width, BLK), F32)],
    )


def first_back_kernel(
    tab_ref, g_ref, h0_ref, h1_ref, w_ref, ea_ref, gain_ref, shift_ref, gain_acc, shift_acc, e_ref, *, per
):
    clear_first(gain_acc, shift_acc)
    rows = w_ref.shape[0]
    e_ref[...] = dot_nn(w_ref[...], g_ref[...])
    places = slot_places(tab_ref, rows, per)
    loads = [lambda at, ref=ref: ref[at, :].astype(F32) for ref in (h0_ref, h1_ref)]
    stats = [norm_stats(load, rows, BLK) for load in loads]

    def finish(at, carry):
        e = e_ref[at, :]
        store_slots(ea_ref, places, at, e)
        total = jnp.zeros((at.size, BLK), F32)
        for j, (load, (mean, rstd)) in enumerate(zip(loads, stats)):
            total = total + e[:, j * BLK : (j + 1) * BLK] * ((load(at) - mean) * rstd)
        gain_acc[at, :] += total
        shift_acc[at, :] += e[:, :BLK] + e[:, BLK:]
        return carry

    sweep(rows, finish, 0)

    @pl.when(pl.program_id(0) == pl.num_programs(0) - 1)
    def _():
        gain_ref[...] = jnp.sum(gain_acc[...], axis=1, keepdims=True)
        shift_ref[...] = jnp.sum(shift_acc[...], axis=1, keepdims=True)


def first_back_call(tab, g_mixed, hidden_all, w, shards):
    width = w.shape[0]
    inner, group = g_mixed.shape
    tok = group // shards
    per = tok // BLK
    return call(
        functools.partial(first_back_kernel, per=per),
        (tab,),
        (group // TILE,),
        [
            (g_mixed, tokens(inner)),
            (hidden_all, slot_block(width, per, 0)),
            (hidden_all, slot_block(width, per, 1)),
            (w, whole(w)),
        ],
        [
            ((shards * width, tok), BF, fixed((shards * width, tok))),
            ((width, 1), F32, fixed((width, 1))),
            ((width, 1), F32, fixed((width, 1))),
        ],
        [pltpu.VMEM((width, BLK), F32), pltpu.VMEM((width, BLK), F32), pltpu.VMEM((width, TILE), F32)],
        flops=LONG,
    )


def branch_kernel(
    eb_ref, mid_ref, cot_ref, small_ref, w_ref, mg_ref, gb_ref, send_ref, bias_ref, att_ref, *, cuts
):
    rows, tok = mid_ref.shape

    def write(at, value):
        grad = cot_ref[at, :].astype(F32) + value
        mg_ref[at, :] = grad
        low = grad.astype(BF)
        gb_ref[at, :] = low
        bias_ref[at, :] = jnp.sum(low.astype(F32), axis=1, keepdims=True)

    norm_back(
        lambda at: mid_ref[at, :], lambda at: eb_ref[at, :].astype(F32), small_ref, 5, rows, tok, write
    )
    att_ref[...] = dot_nn(w_ref[...], gb_ref[...]).astype(BF)
    send_ref[...] = jnp.zeros_like(send_ref)
    for to, lo, hi in cuts:
        send_ref[to : to + hi - lo, :] = att_ref[lo:hi, :]


def branch_call(e_b_own, middle_own, cot_own, small, w_out, cuts, send_rows):
    width, tok = middle_own.shape
    return call(
        functools.partial(branch_kernel, cuts=cuts),
        (),
        (1,),
        [(x, whole(x)) for x in (e_b_own, middle_own, cot_own, small, w_out)],
        [
            (shape, dtype, fixed(shape))
            for shape, dtype in (
                ((width, tok), F32),
                ((width, tok), BF),
                ((send_rows, tok), BF),
                ((width, 1), F32),
            )
        ],
        [pltpu.VMEM((w_out.shape[0], tok), BF)],
    )


def input_kernel(ea_ref, h_ref, mg_ref, small_ref, out_ref):
    def write(at, value):
        out_ref[at, :] = mg_ref[at, :] + value

    rows, tok = mg_ref.shape
    norm_back(
        lambda at: h_ref[at, :].astype(F32),
        lambda at: ea_ref[at, :].astype(F32),
        small_ref,
        0,
        rows,
        tok,
        write,
    )


def input_call(e_a_own, hidden_own, middle_grad, small):
    shape = middle_grad.shape
    return call(
        input_kernel,
        (),
        (1,),
        [(x, whole(x)) for x in (e_a_own, hidden_own, middle_grad, small)],
        [(shape, F32, fixed(shape))],
    )[0]


def half_of(acc_ref, bit, count):
    return acc_ref[pl.ds(pl.multiple_of(bit * count, 8), count), :].astype(BF)


def grad_kernel(core_ref, a_ref, b_ref, small_ref, keep_ref, *refs):
    sends, acc_ref = refs[:-1], refs[-1]
    rows = a_ref.shape[0]
    count = keep_ref.shape[1]
    extra = acc_ref.shape[0] - rows - SMALL_ROWS
    acc_ref[0:rows, :] = dot_nt(a_ref[...], b_ref[...])
    acc_ref[rows : rows + SMALL_ROWS, :] = small_ref[0]
    acc_ref[rows + SMALL_ROWS :, :] = jnp.zeros((extra, acc_ref.shape[1]), F32)
    keep_ref[0] = half_of(acc_ref, core_ref[0], count)
    if len(sends) == 1:
        sends[0][0] = half_of(acc_ref, 1 - core_ref[0], count)
        return
    for n, send_ref in enumerate(sends):

        @pl.when(pl.program_id(0) == n)
        def _(send_ref=send_ref):
            send_ref[...] = half_of(acc_ref, 1 - core_ref[0], count)


def grad_call(core, a, b, small, half, pieces):
    lead, _, cols = small.shape
    rows, group = a.shape[0] // lead, a.shape[1]
    keep = ((lead, half, cols), BF, pl.BlockSpec((1, half, cols), lambda i, *_: (i, 0, 0)))
    outs = call(
        grad_kernel,
        (core,),
        (lead,),
        [
            (a, pl.BlockSpec((rows, group), lambda i, *_: (i, 0))),
            (b, whole(b)),
            (small, pl.BlockSpec((1, SMALL_ROWS, cols), lambda i, *_: (i, 0, 0))),
        ],
        [keep] + ([((half, cols), BF, fixed((half, cols)))] * lead if pieces else [keep]),
        [pltpu.VMEM((2 * half, cols), F32)],
    )
    return outs[0], outs[1:] if pieces else outs[1]


def first_step_kernel(bit_ref, *refs, leads):
    ins, (keep_ref, send_ref, acc_ref) = refs[:-3], refs[-3:]
    count = keep_ref.shape[1]
    first = at = 0
    for lead in leads:
        for n in range(lead):

            @pl.when(pl.program_id(0) == first + n)
            def _(x_ref=ins[at], y_ref=ins[at + 1 + n]):
                acc_ref[...] = x_ref[0].astype(F32) + y_ref[...].astype(F32)

        first += lead
        at += 1 + lead
    keep_ref[0] = half_of(acc_ref, bit_ref[0], count)
    send_ref[0] = half_of(acc_ref, 1 - bit_ref[0], count)


def first_step_call(bit, sums):
    _, count, cols = sums[0][0].shape
    leads = [x.shape[0] for x, _ in sums]
    total = sum(leads)
    ins = []
    first = 0
    for (x, pieces), lead in zip(sums, leads):
        at = lambda i, *_, first=first, lead=lead: (jnp.clip(i - first, 0, lead - 1), 0, 0)
        ins.append((x, pl.BlockSpec((1, count, cols), at)))
        ins += [(y, whole(y)) for y in pieces]
        first += lead
    part = ((total, count // 2, cols), BF, pl.BlockSpec((1, count // 2, cols), lambda i, *_: (i, 0, 0)))
    return call(
        functools.partial(first_step_kernel, leads=leads),
        (bit,),
        (total,),
        ins,
        [part, part],
        [pltpu.VMEM((count, cols), F32)],
    )


def wide_step_kernel(bit_ref, *refs, wide):
    ins, (keep_ref, send_ref, acc_ref) = refs[:-3], refs[-3:]
    count = keep_ref.shape[1]
    end = 0
    for n, (lo, hi) in enumerate(wide):
        if lo > end:
            acc_ref[:, end:lo] = jnp.zeros((acc_ref.shape[0], lo - end), F32)
        end = hi
        acc_ref[:, lo:hi] = ins[2 * n][0].astype(F32) + ins[2 * n + 1][0].astype(F32)
    keep_ref[0] = half_of(acc_ref, bit_ref[0], count)
    send_ref[0] = half_of(acc_ref, 1 - bit_ref[0], count)


def wide_step_call(bit, sums, offsets, cols):
    lead, count, _ = sums[0][0].shape
    ins, wide = [], []
    for (x, y), lo in zip(sums, offsets):
        wide.append((lo, lo + x.shape[2]))
        ins += [(z, pl.BlockSpec((1, count, z.shape[2]), lambda i, *_: (i, 0, 0))) for z in (x, y)]
    part = ((lead, count // 2, cols), BF, pl.BlockSpec((1, count // 2, cols), lambda i, *_: (i, 0, 0)))
    return call(
        functools.partial(wide_step_kernel, wide=wide),
        (bit,),
        (lead,),
        ins,
        [part, part],
        [pltpu.VMEM((count, cols), F32)],
        flops=SHORT,
    )


def step_kernel(bit_ref, x_ref, y_ref, keep_ref, send_ref, acc_ref):
    count = keep_ref.shape[1]
    acc_ref[...] = x_ref[0].astype(F32) + y_ref[0].astype(F32)
    keep_ref[0] = half_of(acc_ref, bit_ref[0], count)
    send_ref[0] = half_of(acc_ref, 1 - bit_ref[0], count)


def step_call(bit, x, y, flops):
    lead, count, cols = x.shape
    block = pl.BlockSpec((1, count, cols), lambda i, *_: (i, 0, 0))
    part = ((lead, count // 2, cols), BF, pl.BlockSpec((1, count // 2, cols), lambda i, *_: (i, 0, 0)))
    return call(
        step_kernel, (bit,), (lead,), [(x, block), (y, block)], [part, part], [pltpu.VMEM((count, cols), F32)], flops
    )


def place_kernel(at_ref, mine_ref, theirs_ref, *refs, spans):
    outs, acc_ref = refs[:-1], refs[-1]
    pieces, _, count, _ = mine_ref.shape
    rows = outs[0].shape[1]
    for n in range(2 * pieces):
        at = pl.multiple_of(at_ref[n], 8)
        acc_ref[pl.ds(at, count), :] = (theirs_ref if n >= pieces else mine_ref)[n % pieces, 0].astype(F32)
    for n, (lo, hi) in enumerate(spans):
        outs[2 * n][0] = acc_ref[0:rows, lo:hi]
        outs[2 * n + 1][0] = acc_ref[rows : rows + SMALL_ROWS, lo:hi]


def place_call(places, mine, theirs, rows, spans):
    pieces, lead, count, cols = mine.shape
    cut = 1280 if cols % 1280 == 0 and len(spans) == 1 else cols
    block = pl.BlockSpec((pieces, 1, count, cut), lambda i, j, *_: (0, i, 0, j))
    outs = []
    for lo, hi in spans:
        lanes = min(hi - lo, cut)
        for height in (rows, SMALL_ROWS):
            spec = pl.BlockSpec((1, height, lanes), lambda i, j, *_: (i, 0, j))
            outs.append(((lead, height, hi - lo), F32, spec))
    inner = [(0, cut)] if len(spans) == 1 else spans
    return call(
        functools.partial(place_kernel, spans=inner),
        (places,),
        (lead, cols // cut),
        [(mine, block), (theirs, block)],
        outs,
        [pltpu.VMEM((2 * pieces * count, cut), F32)],
        flops=SHORT,
    )


ROOT = 0.7978845608028654
CUBE = 0.044715


def gelu(u):
    return 0.5 * u * (1.0 + jnp.tanh(ROOT * (u + CUBE * u * u * u)))


def gelu_slope(u):
    bend = jnp.tanh(ROOT * (u + CUBE * u * u * u))
    return 0.5 * (1.0 + bend) + 0.5 * u * (1.0 - bend * bend) * (ROOT * (1.0 + 3.0 * CUBE * u * u))


def token_sum(values_in):
    return jnp.sum(values_in.astype(F32), axis=1)


def after(x, *first):
    return lax.optimization_barrier((x,) + first)[0]


def together(*values):
    return lax.optimization_barrier(values)


def per_device(
    chips,
    shards,
    hidden_in,
    cotangent,
    slot_index,
    seq_lengths,
    attn_gain,
    attn_shift,
    attn_weight,
    query_bias,
    value_bias,
    out_weight,
    out_bias,
    mlp_gain,
    mlp_shift,
    up_weight,
    up_bias,
    down_weight,
    down_bias,
):
    tok, width = hidden_in.shape
    group = slot_index.shape[0]
    head = width // H
    rows = width // shards
    ff_own = down_weight.shape[0]
    counts, starts, windows, win = head_plan(shards)
    wc = win * head
    reps = 2 * chips
    piece = -(-(rows + SMALL_ROWS) // (8 * reps)) * 8
    half = chips * piece
    me = lax.axis_index("shard")
    chip = lax.axis_index("chip")
    core = lax.axis_index("core")
    blocks = group // BLK
    own_blocks = tok // BLK
    spans = []
    for s in range(shards):
        lo = (starts[s] - windows[s]) * head
        spans.append((s * wc + lo, s * wc + lo + counts[s] * head))

    def to_next(x, t):
        return lax.ppermute(x, "shard", [(i, (i + t) % shards) for i in range(shards)])

    def other_core(x):
        return lax.ppermute(x, "core", [(0, 1), (1, 0)])

    def pick(x, at):
        return lax.dynamic_index_in_dim(x, at, 0, keepdims=False)

    def turn(j):
        return lax.rem(j + 2 * shards, shards)

    def exchange(send):
        got = [pick(send, me)]
        for t in range(1, shards):
            got.append(to_next(pick(send, turn(me + t)), t))
        got = jnp.stack(got)
        return jnp.stack([pick(got, turn(me - j)) for j in range(shards)])

    def over_shard(x):
        return lax.all_gather(x, "shard", axis=0, tiled=True)

    def window(x, s):
        return x[..., windows[s] * head : windows[s] * head + wc]

    def scalar(x):
        return jnp.reshape(x, (1,)).astype(jnp.int32)

    square = chips == 4
    bits = (chip // 2, chip % 2)
    first_bit = jnp.where(core == 0, bits[1], bits[0])
    second_bit = jnp.where(core == 0, bits[0], bits[1])
    slot = 2 * first_bit + second_bit if square else chip
    other_slot = 2 * second_bit + first_bit

    def flip(x, step):
        pairs = []
        for q in range(chips):
            for c in range(2):
                partner = q ^ 1 if (c + step) % 2 == 0 else q ^ 2
                pairs.append((2 * q + c, 2 * partner + c))
        return lax.ppermute(x, ("chip", "core"), pairs)

    def add_low(x, y):
        return (x.astype(F32) + y.astype(F32)).astype(BF)

    def sum_start(a, b, small, *first, pieces=False):
        keep, sends = grad_call(after(scalar(core), *first), a, b, small, half, pieces)
        return keep, [other_core(x) for x in sends] if pieces else other_core(sends)

    def chip_sum(state):
        x = add_low(state[0], jnp.stack(state[1]) if isinstance(state[1], list) else state[1])
        x = jnp.swapaxes(x.reshape(x.shape[0], chips, piece, x.shape[2]), 0, 1)
        return lax.psum_scatter(x, "chip", scatter_dimension=0, tiled=False)

    def sum_second(state, *first, flops=1024):
        if not square:
            return state
        keep, send = step_call(after(scalar(second_bit), *first), *state, flops)
        return keep, flip(send, 1)

    def sum_last(state):
        return add_low(*state) if square else state[0]

    def spread_near(x):
        return jnp.stack([x, flip(x, 1)]) if square else x

    def spread_far(x):
        if not square:
            return lax.all_gather(x, "chip", axis=0, tiled=False)
        return jnp.concatenate([x, flip(x, 0)], axis=0)

    def spread_last(mine, spans, *first):
        places = []
        for c, at in ((core, slot), (1 - core, other_slot)):
            for j in range(chips):
                places.append(c * half + ((at ^ j) if square else j) * piece)
        places = after(jnp.stack(places).astype(jnp.int32), *first)
        return place_call(places, mine, other_core(mine), rows, spans)

    def in_order(bit, x, y):
        return jnp.concatenate([jnp.where(bit == 0, x, y), jnp.where(bit == 0, y, x)], axis=1)

    def my_piece(x):
        x = jnp.pad(x, ((0, 2 * half - x.shape[0]), (0, 0)))
        return lax.dynamic_slice_in_dim(x, core * half + slot * piece, piece, 0)

    def weight_near(x):
        return in_order(second_bit, x, flip(x, 1)) if square else x

    def weight_far(x, *first):
        if not square:
            x = jnp.swapaxes(lax.all_gather(x, "chip", axis=0, tiled=False), 0, 1)
            return x.reshape(x.shape[0], -1, x.shape[-1])
        return in_order(first_bit, after(x, *first) if first else x, flip(x, 0))

    def weight_rows(x):
        x = in_order(core, x, other_core(x))
        return x[:, :rows].reshape(shards * rows, x.shape[-1])

    def small_block(vectors, cols):
        x = jnp.stack(vectors).reshape(len(vectors), shards, rows)
        pad = ((0, 0), (0, SMALL_ROWS - len(vectors)), (0, cols - rows))
        return jnp.pad(jnp.swapaxes(x, 0, 1), pad)

    def with_sum(x, got):
        total = jnp.sum(got[:, :, :rows].astype(F32), axis=0).astype(BF)
        total = jnp.pad(total, ((0, 0), (0, x.shape[1] - rows)))
        row = core * half + slot * piece + lax.broadcasted_iota(jnp.int32, (piece, 1), 0)
        return jnp.where(row >= rows, total, x)[None]

    pos = (slot_index.reshape(blocks, BLK)[:, 0] // BLK).astype(jnp.int32)
    ids = jnp.arange(blocks, dtype=jnp.int32)
    tab = jnp.sum(jnp.where(pos[None, :] == ids[:, None], ids[None, :], 0), axis=1).astype(jnp.int32)
    first_len = seq_lengths[0, :1]

    hidden_own = hidden_in.T
    cot_own = cotangent.T
    small = jnp.stack(
        [attn_gain, attn_shift, query_bias, value_bias, out_bias, mlp_gain, mlp_shift, down_bias]
    )
    small = jnp.pad(small, ((0, 0), (0, 3 * wc - rows)))
    attn_piece = my_piece(attn_weight)
    parts = []
    for s in range(shards):
        cut = [window(attn_piece[:, j * width : (j + 1) * width], s) for j in range(3)]
        parts.append(jnp.concatenate([jnp.concatenate(cut, axis=1), small], axis=0))
    attn_got = exchange(jnp.stack(parts))
    small = jnp.swapaxes(attn_got[:, piece:, :rows], 0, 1).reshape(SMALL_ROWS, width)
    small = small.astype(F32).T
    hidden_all = over_shard(hidden_own)
    attn_near = after(weight_near(attn_got[:, :piece]), hidden_all)
    attn_far = weight_far(attn_near)
    normed_a, hidden = first_norm_call(tab, hidden_all, small, shards)
    w_qkv = weight_rows(after(attn_far, normed_a))
    out_piece = after(my_piece(out_weight), hidden_all)
    out_got = exchange(jnp.stack([out_piece] * shards))
    out_near = weight_near(after(out_got, attn_far))
    up_piece = after(my_piece(up_weight), out_got)
    up_got = exchange(jnp.stack([up_piece[:, s * ff_own : (s + 1) * ff_own] for s in range(shards)]))

    bias_rows = jnp.stack(
        [
            jnp.concatenate(
                [window(small[:, 2], s), jnp.zeros((wc,), F32), window(small[:, 3], s)]
            )
            for s in range(shards)
        ]
    )
    bias_qkv = after(pick(bias_rows, me)[:, None], up_got)
    qkv = (dot_tn(w_qkv, normed_a) + bias_qkv).astype(BF)
    w_out = weight_rows(weight_far(out_near, qkv))
    attended, attended_low, lse = attend(after(first_len, w_out), qkv, win)
    att_all = over_shard(attended_low)
    up_near = weight_near(after(up_got, attended_low))
    w_up = weight_rows(weight_far(after(up_near, att_all)))

    cot_all = over_shard(after(cot_own, att_all))
    att_full = jnp.concatenate([att_all[lo:hi] for lo, hi in spans], axis=0)
    middle = hidden.astype(F32) + dot_tn(w_out, att_full) + small[:, 4:5]
    average = jnp.mean(middle, axis=0, keepdims=True)
    centred = middle - average
    variance = jnp.mean(centred * centred, axis=0, keepdims=True)
    x_b = centred * lax.rsqrt(variance + EPSILON)
    normed_b = (x_b * small[:, 5:6] + small[:, 6:7]).astype(BF)
    x_b = x_b.astype(BF)

    def own_tokens(x):
        parts = [
            lax.dynamic_slice_in_dim(x, pos[me * own_blocks + j] * BLK, BLK, 1)
            for j in range(own_blocks)
        ]
        return jnp.concatenate(parts, axis=1)

    pre = dot_tn(w_up, normed_b) + up_bias.astype(F32)[:, None]
    act = gelu(pre).astype(BF)
    ffn_part = split_call(tab, dot_tn(down_weight, act).astype(BF), shards)
    ffn_chunks = ffn_part.reshape(shards, width, tok)

    def ffn_send(t, part, *first):
        return to_next(after(pick(ffn_chunks, turn(me + t))[part], *first), t)

    ffn_own = pick(ffn_chunks, me).astype(F32)
    ffn_near = ffn_send(1, slice(None))
    cot = join_blocks(after(pos, ffn_part), cot_all, shards)
    g_pre = (dot_nn(down_weight, cot) * gelu_slope(pre)).astype(BF)
    e_b = dot_nn(w_up, g_pre) + after(jnp.zeros((), F32), ffn_near)
    e_b, g_mlp_gain, g_mlp_shift = split_sums_call(tab, e_b, x_b, shards)
    ffn_own = ffn_own + ffn_near.astype(F32)
    middle_own = own_tokens(after(middle, e_b))
    g_up_bias = token_sum(after(g_pre, e_b))[:, None]

    def token_scatter(x):
        return lax.psum_scatter(x, "shard", scatter_dimension=0, tiled=True)

    e_b_own = token_scatter(e_b)
    lead = ff_own // rows
    small_down = jnp.pad(
        g_up_bias[:, 0][None, None], ((0, lead - 1), (0, SMALL_ROWS - 1), (0, width - ff_own))
    )
    down_sum = sum_start(act, cot, small_down, e_b, pieces=True)
    small_up = small_block([g_mlp_gain[:, 0], g_mlp_shift[:, 0], token_sum(cot_own)], ff_own)
    up_sum = sum_start(normed_b, g_pre, small_up, down_sum[0], pieces=True)
    merged = square and ff_own == width
    if merged:
        keep, send = first_step_call(scalar(first_bit), [down_sum, up_sum])
        ffn_sum = (keep, flip(send, 0))
    else:
        ffn_sum = (chip_sum(down_sum), chip_sum(up_sum))
    e_b_own, keep = together(e_b_own, ffn_sum[0])
    ffn_sum = (keep,) + ffn_sum[1:]

    cuts = [(lo, lo - s * wc + windows[s] * head, hi - s * wc + windows[s] * head) for s, (lo, hi) in enumerate(spans)]
    middle_grad, g_branch, sends, g_out_bias = branch_call(
        e_b_own, middle_own, cot_own, small, w_out, cuts, shards * wc
    )
    g_att = exchange(sends.reshape(shards, wc, tok)).reshape(shards * wc, tok)
    att_own = own_tokens(att_full)
    if merged:
        ffn_sum = sum_second(ffn_sum, sends)
    out_sum = sum_start(att_own, g_branch, small_block([g_out_bias[:, 0]], width), ffn_sum[0])
    keep_out = out_sum[0]
    ffn_back = ffn_send(shards - 1, slice(None), g_att)
    g_att = join_blocks(pos, g_att, shards)
    g_mixed = attend_back(first_len, qkv, g_att, attended, lse, win)
    g_mixed_rows = g_mixed.reshape(3 * wc, group)

    e_a, g_attn_gain, g_attn_shift = first_back_call(
        after(tab, keep_out, ffn_back), g_mixed_rows, hidden_all, w_qkv, shards
    )
    e_a_own = token_scatter(e_a)
    ffn_own = ffn_own + ffn_back.astype(F32)
    if merged:
        ffn_last = after(sum_last(ffn_sum), e_a)
        down_own, up_own = ffn_last[:lead], ffn_last[lead:]
    else:
        down_own, up_own = ffn_sum
    up_got = exchange(up_own)
    down_near = spread_near(down_own)
    up_row = with_sum(jnp.concatenate([up_got[s] for s in range(shards)], axis=-1), up_got)
    up_near = spread_near(up_row)
    cut = width // 2
    ffn_top = [ffn_send(t, slice(0, cut), e_a_own) for t in range(2, shards - 1)]
    ffn_low = [ffn_send(t, slice(cut, None), *ffn_top) for t in range(2, shards - 1)]
    for top, low in zip(ffn_top, ffn_low):
        ffn_own = ffn_own + jnp.concatenate([top, low], axis=0).astype(F32)

    def place(x):
        outs = [
            jnp.pad(x, (windows[s] * head, width - windows[s] * head - wc)) for s in range(shards)
        ]
        return pick(jnp.stack(outs), me)

    sums = jnp.sum(g_mixed.astype(F32), axis=2)
    small_mix = small_block(
        [g_attn_gain[:, 0], g_attn_shift[:, 0], place(sums[0]), place(sums[2])], 3 * wc
    )
    mix_sum = sum_start(normed_a, g_mixed_rows, small_mix)
    down_mine = spread_far(down_near)

    skip = -(-width // BLK) * BLK
    if square:
        keep, send = wide_step_call(
            after(scalar(first_bit), down_near), [(keep_out, out_sum[1]), mix_sum], (0, skip), skip + 3 * wc
        )
        wide_sum = sum_second((keep, flip(send, 0)), up_near, *ffn_top, flops=SHORT)
        wide_own = sum_last(wide_sum)
    else:
        gap = jnp.zeros((shards, piece, skip - width), BF)
        wide_own = jnp.concatenate([chip_sum((keep_out, out_sum[1])), gap, chip_sum(mix_sum)], axis=-1)
    wide_own = after(wide_own, e_a_own, *ffn_low)
    wide_got = exchange(wide_own)
    up_mine = spread_far(after(up_near, wide_own))
    g_down_full, down_small = spread_last(down_mine, [(0, width)], wide_own)
    g_up_full, up_small = spread_last(up_mine, [(0, shards * ff_own)])
    columns = []
    for j in range(3):
        for s in range(shards):
            lo, hi = skip + j * wc + spans[s][0] - s * wc, skip + j * wc + spans[s][1] - s * wc
            columns.append(wide_got[s, :, lo:hi])
    mix_row = with_sum(jnp.concatenate(columns, axis=-1), wide_got[:, :, skip:])
    out_row = jnp.sum(wide_got[:, :, :skip].astype(F32), axis=0).astype(BF)
    wide_row = jnp.concatenate([out_row[None], mix_row], axis=-1)
    wide_near = spread_near(after(wide_row, g_down_full))
    g_out_full, out_small, g_mix_full, mix_small = spread_last(
        spread_far(wide_near), [(0, width), (skip, skip + 3 * width)]
    )

    block_out = (middle_own + ffn_own + small[:, 7:8]).astype(BF).T
    input_grad = input_call(e_a_own, hidden_own, middle_grad, small).T

    return (
        block_out,
        input_grad,
        mix_small[0, 0, :rows],
        mix_small[0, 1, :rows],
        g_mix_full[0],
        mix_small[0, 2, :rows],
        mix_small[0, 3, :rows],
        g_out_full[0],
        out_small[0, 0, :rows],
        up_small[0, 0, :rows],
        up_small[0, 1, :rows],
        g_up_full[0],
        down_small[0, 0, :ff_own],
        g_down_full.reshape(ff_own, width),
        up_small[0, 2, :rows],
    )


def solution(mesh):
    reps, shards = mesh.shape["rep"], mesh.shape["shard"]
    fine = Mesh(mesh.devices.reshape(reps // 2, 2, shards), ("chip", "core", "shard"))
    rep = ("chip", "core")
    both = ("chip", "core", "shard")
    return jax.shard_map(
        functools.partial(per_device, reps // 2, shards),
        mesh=fine,
        in_specs=(
            P(both, None),
            P(both, None),
            P(rep),
            P(rep, None),
            P("shard"),
            P("shard"),
            P("shard", None),
            P("shard"),
            P("shard"),
            P("shard", None),
            P("shard"),
            P("shard"),
            P("shard"),
            P("shard", None),
            P("shard"),
            P("shard", None),
            P("shard"),
        ),
        out_specs=(
            P(both, None),
            P(both, None),
            P("shard"),
            P("shard"),
            P("shard", None),
            P("shard"),
            P("shard"),
            P("shard", None),
            P("shard"),
            P("shard"),
            P("shard"),
            P("shard", None),
            P("shard"),
            P("shard", None),
            P("shard"),
        ),
        check_vma=False,
    )
```

```python
import functools

import jax
import jax.numpy as jnp
from jax import lax
from jax.experimental import pallas as pl
from jax.experimental.pallas import tpu as pltpu
from jax.sharding import Mesh
from jax.sharding import PartitionSpec as P

H = 25
BLK = 128
TILE = 256
EPSILON = 1e-05
BF = jnp.bfloat16
F32 = jnp.float32
VMEM_LIMIT = 56 * 1024 * 1024
SMALL_ROWS = 8


def dot_nt(a, b):
    return lax.dot_general(a, b, (((1,), (1,)), ((), ())), preferred_element_type=F32)


def dot_tn(a, b):
    return lax.dot_general(a, b, (((0,), (0,)), ((), ())), preferred_element_type=F32)


def dot_nn(a, b):
    return lax.dot_general(a, b, (((1,), (0,)), ((), ())), preferred_element_type=F32)


def head_plan(shards):
    base, extra = H // shards, H % shards
    counts = [base + (1 if s < extra else 0) for s in range(shards)]
    starts = [sum(counts[:s]) for s in range(shards)]
    width = max(counts)
    windows = [min(st, H - width) for st in starts]
    return counts, starts, windows, width


LONG = 20_000_000_000
SHORT = 10_000_000_000


def call(kernel, scalars, grid, ins, outs, scratch=(), flops=1024):
    return pl.pallas_call(
        kernel,
        out_shape=[jax.ShapeDtypeStruct(shape, dtype) for shape, dtype, _ in outs],
        grid_spec=pltpu.PrefetchScalarGridSpec(
            num_scalar_prefetch=len(scalars),
            grid=grid,
            in_specs=[spec for _, spec in ins],
            out_specs=[spec for _, _, spec in outs],
            scratch_shapes=list(scratch),
        ),
        compiler_params=pltpu.CompilerParams(vmem_limit_bytes=VMEM_LIMIT),
        cost_estimate=pl.CostEstimate(flops=flops, bytes_accessed=1024, transcendentals=0),
    )(*scalars, *[array for array, _ in ins])


def whole(array):
    zeros = (0,) * array.ndim
    return pl.BlockSpec(array.shape, lambda *_: zeros, pipeline_mode=pl.Buffered(1))


def fixed(shape):
    zeros = (0,) * len(shape)
    return pl.BlockSpec(shape, lambda *_: zeros)


def tokens(rows):
    return pl.BlockSpec((rows, TILE), lambda i, *_: (0, i))


def slot_block(rows, per, which):
    return pl.BlockSpec(
        (rows, BLK), lambda i, tab, *_: (tab[2 * i + which] // per, lax.rem(tab[2 * i + which], per))
    )


STEP = 80


def sweep(rows, body, carry, step=STEP):
    while rows % step:
        step -= 16
    for at in range(0, rows, step):
        carry = body(pl.ds(at, step), carry)
    return carry


def chunk(rows, lanes):
    step = STEP
    while rows % step:
        step -= 16
    return jnp.zeros((step, lanes), F32)


def column_mean(acc, rows):
    return jnp.sum(acc, axis=0, keepdims=True) * (1.0 / rows)


def norm_stats(load, rows, lanes):
    zero = chunk(rows, lanes)
    mean = column_mean(sweep(rows, lambda at, acc: acc + load(at), zero), rows)

    def spread(at, acc):
        centred = load(at) - mean
        return acc + centred * centred

    return mean, lax.rsqrt(column_mean(sweep(rows, spread, zero), rows) + EPSILON)


def norm_back(load, load_e, gain_ref, col, rows, lanes, write):
    mean, rstd = norm_stats(load, rows, lanes)
    zero = chunk(rows, lanes)

    def both(at):
        return (load(at) - mean) * rstd, load_e(at) * gain_ref[at, col : col + 1]

    def sums(at, carry):
        x, c = both(at)
        return carry[0] + c, carry[1] + c * x

    mean_c, mean_cx = sweep(rows, sums, (zero, zero))
    mean_c, mean_cx = column_mean(mean_c, rows), column_mean(mean_cx, rows)

    def last(at, carry):
        x, c = both(at)
        write(at, rstd * (c - mean_c - x * mean_cx))
        return carry

    sweep(rows, last, 0)


def slot_places(tab_ref, rows, per):
    places = []
    for which in range(2):
        place = tab_ref[2 * pl.program_id(0) + which]
        row = pl.multiple_of((place // per) * rows, 16)
        places.append((row, pl.multiple_of(lax.rem(place, per) * BLK, BLK)))
    return places


def store_slots(out_ref, places, at, value):
    for which, (row, lane) in enumerate(places):
        rows = pl.ds(pl.multiple_of(row + at.start, 16), at.size)
        out_ref[rows, pl.ds(lane, BLK)] = value[:, which * BLK : (which + 1) * BLK].astype(out_ref.dtype)


def clear_first(*refs):
    @pl.when(pl.program_id(0) == 0)
    def _():
        for ref in refs:
            ref[...] = jnp.zeros_like(ref)


def first_norm_kernel(tab_ref, h0_ref, h1_ref, small_ref, na_ref, pack_ref):
    rows = na_ref.shape[0]
    for j, ref in enumerate((h0_ref, h1_ref)):
        load = lambda at, ref=ref: ref[at, :].astype(F32)
        mean, rstd = norm_stats(load, rows, BLK)

        def write(at, carry, load=load, mean=mean, rstd=rstd, j=j):
            x = (load(at) - mean) * rstd
            na_ref[at, j * BLK : (j + 1) * BLK] = (x * small_ref[at, 0:1] + small_ref[at, 1:2]).astype(BF)
            return carry

        pack_ref[:, j * BLK : (j + 1) * BLK] = ref[...]

        sweep(rows, write, 0)


def first_norm_call(tab, hidden_all, small, shards):
    width, tok = small.shape[0], hidden_all.shape[1]
    group = tok * shards
    per = tok // BLK
    return call(
        first_norm_kernel,
        (tab,),
        (group // TILE,),
        [
            (hidden_all, slot_block(width, per, 0)),
            (hidden_all, slot_block(width, per, 1)),
            (small, whole(small)),
        ],
        [((width, group), BF, tokens(width))] * 2,
        flops=LONG,
    )


def tile_variants(tiles):
    return [(i, st) for i in range(tiles) for st in range(i + 1)]


def allowed_mask(first_len, q_base, k_base, k_rows):
    kpos = k_base + lax.broadcasted_iota(jnp.int32, (k_rows, TILE), 0)
    qrow = q_base + lax.broadcasted_iota(jnp.int32, (1, TILE), 1)
    low = jnp.where(qrow >= first_len, first_len, 0)
    return (kpos <= qrow) & (kpos >= low)


def attend_kernel(len_ref, q_ref, k_ref, v_ref, o_ref, ol_ref, lse_ref, *, tiles):
    first_len = len_ref[0]
    for i, st in tile_variants(tiles):
        q_base = i * TILE
        start = jnp.where(q_base >= first_len, first_len // TILE, 0)

        @pl.when(start == st)
        def _():
            rows = pl.ds(q_base, TILE)
            keys = pl.ds(st * TILE, (i + 1 - st) * TILE)
            ok = allowed_mask(first_len, q_base, st * TILE, (i + 1 - st) * TILE)
            s = dot_tn(k_ref[:, keys], q_ref[:, rows] * jnp.asarray(0.125, BF))
            s = jnp.where(ok, s, -1000000000.0)
            top = jnp.max(s, axis=0, keepdims=True)
            e = jnp.exp(s - top)
            tot = jnp.sum(e, axis=0, keepdims=True)
            soft = (e * (1.0 / tot)).astype(BF)
            o = dot_nn(v_ref[:, keys], soft)
            o_ref[:, rows] = o
            ol_ref[:, rows] = o.astype(BF)
            lse_ref[0, :, rows] = top + jnp.log(tot)


def attend(first_len, qkv, heads):
    group = qkv.shape[1]
    rows = heads * 64
    block = lambda off: pl.BlockSpec((64, group), lambda h, t, off=off: (off + h, 0))
    return call(
        functools.partial(attend_kernel, tiles=group // TILE),
        (first_len,),
        (heads,),
        [(qkv, block(0)), (qkv, block(heads)), (qkv, block(2 * heads))],
        [
            ((rows, group), F32, block(0)),
            ((rows, group), BF, block(0)),
            ((heads, 1, group), F32, pl.BlockSpec((1, 1, group), lambda h, t: (h, 0, 0))),
        ],
        flops=LONG,
    )


def attend_back_kernel(
    len_ref, q_ref, k_ref, v_ref, g_ref, o_ref, lse_ref, out_ref, dk_acc, dv_acc, *, tiles
):
    first_len = len_ref[0]
    dk_acc[...] = jnp.zeros_like(dk_acc)
    dv_acc[...] = jnp.zeros_like(dv_acc)
    for i, st in tile_variants(tiles):
        q_base = i * TILE
        start = jnp.where(q_base >= first_len, first_len // TILE, 0)

        @pl.when(start == st)
        def _():
            rows = pl.ds(q_base, TILE)
            keys = pl.ds(st * TILE, (i + 1 - st) * TILE)
            q = q_ref[:, rows] * jnp.asarray(0.125, BF)
            k = k_ref[:, keys]
            v = v_ref[:, keys]
            g = g_ref[:, rows]
            delta = jnp.sum(g.astype(F32) * o_ref[:, rows], axis=0, keepdims=True)
            ok = allowed_mask(first_len, q_base, st * TILE, (i + 1 - st) * TILE)
            s = dot_tn(k, q)
            soft = jnp.exp(jnp.where(ok, s, -1000000000.0) - lse_ref[0, :, rows])
            dp = dot_tn(v, g)
            ds = (soft * (dp - delta)).astype(BF)
            dv_acc[:, keys] += dot_nt(g, soft.astype(BF))
            dk_acc[:, keys] += dot_nt(q, ds)
            out_ref[0, :, rows] = (dot_nn(k, ds) * 0.125).astype(BF)

    out_ref[1] = dk_acc[...].astype(BF)
    out_ref[2] = dv_acc[...].astype(BF)


def attend_back(first_len, qkv, g, o, lse, heads):
    group = qkv.shape[1]
    rows = heads * 64
    block = lambda off: pl.BlockSpec((64, group), lambda h, t, off=off: (off + h, 0))
    return call(
        functools.partial(attend_back_kernel, tiles=group // TILE),
        (first_len,),
        (heads,),
        [
            (qkv, block(0)),
            (qkv, block(heads)),
            (qkv, block(2 * heads)),
            (g, block(0)),
            (o, block(0)),
            (lse, pl.BlockSpec((1, 1, group), lambda h, t: (h, 0, 0))),
        ],
        [((3, rows, group), BF, pl.BlockSpec((3, 64, group), lambda h, t: (0, h, 0)))],
        [pltpu.VMEM((64, group), F32), pltpu.VMEM((64, group), F32)],
        flops=LONG,
    )[0]


def join_kernel(pos_ref, x_ref, out):
    rows = out.shape[0]
    per = x_ref.shape[1] // BLK
    for j in range(out.shape[1] // BLK):
        at = pl.multiple_of(pos_ref[j] * BLK, BLK)
        chunk = (j // per) * rows
        out[:, pl.ds(at, BLK)] = x_ref[chunk : chunk + rows, (j % per) * BLK : (j % per + 1) * BLK]


def join_blocks(pos, x, count):
    rows, tok = x.shape[0] // count, x.shape[1]
    shape = (rows, count * tok)
    return call(join_kernel, (pos,), (1,), [(x, whole(x))], [(shape, x.dtype, fixed(shape))])[0]


def split_kernel(tab_ref, x_ref, out_ref, *, per):
    rows = x_ref.shape[0]
    store_slots(out_ref, slot_places(tab_ref, rows, per), pl.ds(0, rows), x_ref[...])


def split_call(tab, x, shards):
    width, group = x.shape
    tok = group // shards
    shape = (shards * width, tok)
    return call(
        functools.partial(split_kernel, per=tok // BLK),
        (tab,),
        (group // TILE,),
        [(x, tokens(width))],
        [(shape, BF, fixed(shape))],
    )[0]


def split_sums_kernel(tab_ref, e_ref, xb_ref, out_ref, gain_ref, shift_ref, gain_acc, shift_acc, *, per):
    clear_first(gain_acc, shift_acc)
    rows = e_ref.shape[0]
    places = slot_places(tab_ref, rows, per)

    def finish(at, carry):
        e = e_ref[at, :]
        ex = e * xb_ref[at, :].astype(F32)
        gain_acc[at, :] += ex[:, :BLK] + ex[:, BLK:]
        shift_acc[at, :] += e[:, :BLK] + e[:, BLK:]
        store_slots(out_ref, places, at, e)
        return carry

    sweep(rows, finish, 0)

    @pl.when(pl.program_id(0) == pl.num_programs(0) - 1)
    def _():
        gain_ref[...] = jnp.sum(gain_acc[...], axis=1, keepdims=True)
        shift_ref[...] = jnp.sum(shift_acc[...], axis=1, keepdims=True)


def split_sums_call(tab, e, x, shards):
    width, group = e.shape
    tok = group // shards
    shape = (shards * width, tok)
    return call(
        functools.partial(split_sums_kernel, per=tok // BLK),
        (tab,),
        (group // TILE,),
        [(e, tokens(width)), (x, tokens(width))],
        [(shape, BF, fixed(shape))] + [((width, 1), F32, fixed((width, 1)))] * 2,
        [pltpu.VMEM((width, BLK), F32), pltpu.VMEM((width, BLK), F32)],
    )


def first_back_kernel(
    tab_ref, g_ref, h0_ref, h1_ref, w_ref, ea_ref, gain_ref, shift_ref, gain_acc, shift_acc, e_ref, *, per
):
    clear_first(gain_acc, shift_acc)
    rows = w_ref.shape[0]
    e_ref[...] = dot_nn(w_ref[...], g_ref[...])
    places = slot_places(tab_ref, rows, per)
    loads = [lambda at, ref=ref: ref[at, :].astype(F32) for ref in (h0_ref, h1_ref)]
    stats = [norm_stats(load, rows, BLK) for load in loads]

    def finish(at, carry):
        e = e_ref[at, :]
        store_slots(ea_ref, places, at, e)
        total = jnp.zeros((at.size, BLK), F32)
        for j, (load, (mean, rstd)) in enumerate(zip(loads, stats)):
            total = total + e[:, j * BLK : (j + 1) * BLK] * ((load(at) - mean) * rstd)
        gain_acc[at, :] += total
        shift_acc[at, :] += e[:, :BLK] + e[:, BLK:]
        return carry

    sweep(rows, finish, 0)

    @pl.when(pl.program_id(0) == pl.num_programs(0) - 1)
    def _():
        gain_ref[...] = jnp.sum(gain_acc[...], axis=1, keepdims=True)
        shift_ref[...] = jnp.sum(shift_acc[...], axis=1, keepdims=True)


def first_back_call(tab, g_mixed, hidden_all, w, shards):
    width = w.shape[0]
    inner, group = g_mixed.shape
    tok = group // shards
    per = tok // BLK
    return call(
        functools.partial(first_back_kernel, per=per),
        (tab,),
        (group // TILE,),
        [
            (g_mixed, tokens(inner)),
            (hidden_all, slot_block(width, per, 0)),
            (hidden_all, slot_block(width, per, 1)),
            (w, whole(w)),
        ],
        [
            ((shards * width, tok), BF, fixed((shards * width, tok))),
            ((width, 1), F32, fixed((width, 1))),
            ((width, 1), F32, fixed((width, 1))),
        ],
        [pltpu.VMEM((width, BLK), F32), pltpu.VMEM((width, BLK), F32), pltpu.VMEM((width, TILE), F32)],
        flops=LONG,
    )


def branch_kernel(
    eb_ref, mid_ref, cot_ref, small_ref, w_ref, mg_ref, gb_ref, send_ref, bias_ref, att_ref, *, cuts
):
    rows, tok = mid_ref.shape

    def write(at, value):
        grad = cot_ref[at, :].astype(F32) + value
        mg_ref[at, :] = grad
        low = grad.astype(BF)
        gb_ref[at, :] = low
        bias_ref[at, :] = jnp.sum(low.astype(F32), axis=1, keepdims=True)

    norm_back(
        lambda at: mid_ref[at, :], lambda at: eb_ref[at, :].astype(F32), small_ref, 5, rows, tok, write
    )
    att_ref[...] = dot_nn(w_ref[...], gb_ref[...]).astype(BF)
    send_ref[...] = jnp.zeros_like(send_ref)
    for to, lo, hi in cuts:
        send_ref[to : to + hi - lo, :] = att_ref[lo:hi, :]


def branch_call(e_b_own, middle_own, cot_own, small, w_out, cuts, send_rows):
    width, tok = middle_own.shape
    return call(
        functools.partial(branch_kernel, cuts=cuts),
        (),
        (1,),
        [(x, whole(x)) for x in (e_b_own, middle_own, cot_own, small, w_out)],
        [
            (shape, dtype, fixed(shape))
            for shape, dtype in (
                ((width, tok), F32),
                ((width, tok), BF),
                ((send_rows, tok), BF),
                ((width, 1), F32),
            )
        ],
        [pltpu.VMEM((w_out.shape[0], tok), BF)],
    )


def input_kernel(ea_ref, h_ref, mg_ref, small_ref, out_ref):
    def write(at, value):
        out_ref[at, :] = mg_ref[at, :] + value

    rows, tok = mg_ref.shape
    norm_back(
        lambda at: h_ref[at, :].astype(F32),
        lambda at: ea_ref[at, :].astype(F32),
        small_ref,
        0,
        rows,
        tok,
        write,
    )


def input_call(e_a_own, hidden_own, middle_grad, small):
    shape = middle_grad.shape
    return call(
        input_kernel,
        (),
        (1,),
        [(x, whole(x)) for x in (e_a_own, hidden_own, middle_grad, small)],
        [(shape, F32, fixed(shape))],
    )[0]


def half_of(acc_ref, bit, count):
    return acc_ref[pl.ds(pl.multiple_of(bit * count, 8), count), :].astype(BF)


def grad_kernel(core_ref, a_ref, b_ref, small_ref, keep_ref, *refs):
    sends, acc_ref = refs[:-1], refs[-1]
    rows = a_ref.shape[0]
    count = keep_ref.shape[1]
    extra = acc_ref.shape[0] - rows - SMALL_ROWS
    acc_ref[0:rows, :] = dot_nt(a_ref[...], b_ref[...])
    acc_ref[rows : rows + SMALL_ROWS, :] = small_ref[0]
    acc_ref[rows + SMALL_ROWS :, :] = jnp.zeros((extra, acc_ref.shape[1]), F32)
    keep_ref[0] = half_of(acc_ref, core_ref[0], count)
    if len(sends) == 1:
        sends[0][0] = half_of(acc_ref, 1 - core_ref[0], count)
        return
    for n, send_ref in enumerate(sends):

        @pl.when(pl.program_id(0) == n)
        def _(send_ref=send_ref):
            send_ref[...] = half_of(acc_ref, 1 - core_ref[0], count)


def grad_call(core, a, b, small, half, pieces):
    lead, _, cols = small.shape
    rows, group = a.shape[0] // lead, a.shape[1]
    keep = ((lead, half, cols), BF, pl.BlockSpec((1, half, cols), lambda i, *_: (i, 0, 0)))
    outs = call(
        grad_kernel,
        (core,),
        (lead,),
        [
            (a, pl.BlockSpec((rows, group), lambda i, *_: (i, 0))),
            (b, whole(b)),
            (small, pl.BlockSpec((1, SMALL_ROWS, cols), lambda i, *_: (i, 0, 0))),
        ],
        [keep] + ([((half, cols), BF, fixed((half, cols)))] * lead if pieces else [keep]),
        [pltpu.VMEM((2 * half, cols), F32)],
    )
    return outs[0], outs[1:] if pieces else outs[1]


def first_step_kernel(bit_ref, *refs, leads):
    ins, (keep_ref, send_ref, acc_ref) = refs[:-3], refs[-3:]
    count = keep_ref.shape[1]
    first = at = 0
    for lead in leads:
        for n in range(lead):

            @pl.when(pl.program_id(0) == first + n)
            def _(x_ref=ins[at], y_ref=ins[at + 1 + n]):
                acc_ref[...] = x_ref[0].astype(F32) + y_ref[...].astype(F32)

        first += lead
        at += 1 + lead
    keep_ref[0] = half_of(acc_ref, bit_ref[0], count)
    send_ref[0] = half_of(acc_ref, 1 - bit_ref[0], count)


def first_step_call(bit, sums):
    _, count, cols = sums[0][0].shape
    leads = [x.shape[0] for x, _ in sums]
    total = sum(leads)
    ins = []
    first = 0
    for (x, pieces), lead in zip(sums, leads):
        at = lambda i, *_, first=first, lead=lead: (jnp.clip(i - first, 0, lead - 1), 0, 0)
        ins.append((x, pl.BlockSpec((1, count, cols), at)))
        ins += [(y, whole(y)) for y in pieces]
        first += lead
    part = ((total, count // 2, cols), BF, pl.BlockSpec((1, count // 2, cols), lambda i, *_: (i, 0, 0)))
    return call(
        functools.partial(first_step_kernel, leads=leads),
        (bit,),
        (total,),
        ins,
        [part, part],
        [pltpu.VMEM((count, cols), F32)],
    )


def wide_step_kernel(bit_ref, *refs, wide):
    ins, (keep_ref, send_ref, acc_ref) = refs[:-3], refs[-3:]
    count = keep_ref.shape[1]
    end = 0
    for n, (lo, hi) in enumerate(wide):
        if lo > end:
            acc_ref[:, end:lo] = jnp.zeros((acc_ref.shape[0], lo - end), F32)
        end = hi
        acc_ref[:, lo:hi] = ins[2 * n][0].astype(F32) + ins[2 * n + 1][0].astype(F32)
    keep_ref[0] = half_of(acc_ref, bit_ref[0], count)
    send_ref[0] = half_of(acc_ref, 1 - bit_ref[0], count)


def wide_step_call(bit, sums, offsets, cols):
    lead, count, _ = sums[0][0].shape
    ins, wide = [], []
    for (x, y), lo in zip(sums, offsets):
        wide.append((lo, lo + x.shape[2]))
        ins += [(z, pl.BlockSpec((1, count, z.shape[2]), lambda i, *_: (i, 0, 0))) for z in (x, y)]
    part = ((lead, count // 2, cols), BF, pl.BlockSpec((1, count // 2, cols), lambda i, *_: (i, 0, 0)))
    return call(
        functools.partial(wide_step_kernel, wide=wide),
        (bit,),
        (lead,),
        ins,
        [part, part],
        [pltpu.VMEM((count, cols), F32)],
        flops=SHORT,
    )


def step_kernel(bit_ref, x_ref, y_ref, keep_ref, send_ref, acc_ref):
    count = keep_ref.shape[1]
    acc_ref[...] = x_ref[0].astype(F32) + y_ref[0].astype(F32)
    keep_ref[0] = half_of(acc_ref, bit_ref[0], count)
    send_ref[0] = half_of(acc_ref, 1 - bit_ref[0], count)


def step_call(bit, x, y, flops):
    lead, count, cols = x.shape
    block = pl.BlockSpec((1, count, cols), lambda i, *_: (i, 0, 0))
    part = ((lead, count // 2, cols), BF, pl.BlockSpec((1, count // 2, cols), lambda i, *_: (i, 0, 0)))
    return call(
        step_kernel, (bit,), (lead,), [(x, block), (y, block)], [part, part], [pltpu.VMEM((count, cols), F32)], flops
    )


def place_kernel(at_ref, mine_ref, theirs_ref, *refs, spans):
    outs, acc_ref = refs[:-1], refs[-1]
    pieces, _, count, _ = mine_ref.shape
    rows = outs[0].shape[1]
    for n in range(2 * pieces):
        at = pl.multiple_of(at_ref[n], 8)
        acc_ref[pl.ds(at, count), :] = (theirs_ref if n >= pieces else mine_ref)[n % pieces, 0].astype(F32)
    for n, (lo, hi) in enumerate(spans):
        outs[2 * n][0] = acc_ref[0:rows, lo:hi]
        outs[2 * n + 1][0] = acc_ref[rows : rows + SMALL_ROWS, lo:hi]


def place_call(places, mine, theirs, rows, spans):
    pieces, lead, count, cols = mine.shape
    cut = 1280 if cols % 1280 == 0 and len(spans) == 1 else cols
    block = pl.BlockSpec((pieces, 1, count, cut), lambda i, j, *_: (0, i, 0, j))
    outs = []
    for lo, hi in spans:
        lanes = min(hi - lo, cut)
        for height in (rows, SMALL_ROWS):
            spec = pl.BlockSpec((1, height, lanes), lambda i, j, *_: (i, 0, j))
            outs.append(((lead, height, hi - lo), F32, spec))
    inner = [(0, cut)] if len(spans) == 1 else spans
    return call(
        functools.partial(place_kernel, spans=inner),
        (places,),
        (lead, cols // cut),
        [(mine, block), (theirs, block)],
        outs,
        [pltpu.VMEM((2 * pieces * count, cut), F32)],
        flops=SHORT,
    )


ROOT = 0.7978845608028654
CUBE = 0.044715


def gelu(u):
    return 0.5 * u * (1.0 + jnp.tanh(ROOT * (u + CUBE * u * u * u)))


def gelu_slope(u):
    bend = jnp.tanh(ROOT * (u + CUBE * u * u * u))
    return 0.5 * (1.0 + bend) + 0.5 * u * (1.0 - bend * bend) * (ROOT * (1.0 + 3.0 * CUBE * u * u))


def token_sum(values_in):
    return jnp.sum(values_in.astype(F32), axis=1)


def after(x, *first):
    return lax.optimization_barrier((x,) + first)[0]


def together(*values):
    return lax.optimization_barrier(values)


def per_device(
    chips,
    shards,
    hidden_in,
    cotangent,
    slot_index,
    seq_lengths,
    attn_gain,
    attn_shift,
    attn_weight,
    query_bias,
    value_bias,
    out_weight,
    out_bias,
    mlp_gain,
    mlp_shift,
    up_weight,
    up_bias,
    down_weight,
    down_bias,
):
    tok, width = hidden_in.shape
    group = slot_index.shape[0]
    head = width // H
    rows = width // shards
    ff_own = down_weight.shape[0]
    counts, starts, windows, win = head_plan(shards)
    wc = win * head
    reps = 2 * chips
    piece = -(-(rows + SMALL_ROWS) // (8 * reps)) * 8
    half = chips * piece
    me = lax.axis_index("shard")
    chip = lax.axis_index("chip")
    core = lax.axis_index("core")
    blocks = group // BLK
    own_blocks = tok // BLK
    spans = []
    for s in range(shards):
        lo = (starts[s] - windows[s]) * head
        spans.append((s * wc + lo, s * wc + lo + counts[s] * head))

    def to_next(x, t):
        return lax.ppermute(x, "shard", [(i, (i + t) % shards) for i in range(shards)])

    def other_core(x):
        return lax.ppermute(x, "core", [(0, 1), (1, 0)])

    def pick(x, at):
        return lax.dynamic_index_in_dim(x, at, 0, keepdims=False)

    def turn(j):
        return lax.rem(j + 2 * shards, shards)

    def exchange(send):
        got = [pick(send, me)]
        for t in range(1, shards):
            got.append(to_next(pick(send, turn(me + t)), t))
        got = jnp.stack(got)
        return jnp.stack([pick(got, turn(me - j)) for j in range(shards)])

    def over_shard(x):
        return lax.all_gather(x, "shard", axis=0, tiled=True)

    def window(x, s):
        return x[..., windows[s] * head : windows[s] * head + wc]

    def scalar(x):
        return jnp.reshape(x, (1,)).astype(jnp.int32)

    square = chips == 4
    bits = (chip // 2, chip % 2)
    first_bit = jnp.where(core == 0, bits[1], bits[0])
    second_bit = jnp.where(core == 0, bits[0], bits[1])
    slot = 2 * first_bit + second_bit if square else chip
    other_slot = 2 * second_bit + first_bit

    def flip(x, step):
        pairs = []
        for q in range(chips):
            for c in range(2):
                partner = q ^ 1 if (c + step) % 2 == 0 else q ^ 2
                pairs.append((2 * q + c, 2 * partner + c))
        return lax.ppermute(x, ("chip", "core"), pairs)

    def add_low(x, y):
        return (x.astype(F32) + y.astype(F32)).astype(BF)

    def sum_start(a, b, small, *first, pieces=False):
        keep, sends = grad_call(after(scalar(core), *first), a, b, small, half, pieces)
        return keep, [other_core(x) for x in sends] if pieces else other_core(sends)

    def chip_sum(state):
        x = add_low(state[0], jnp.stack(state[1]) if isinstance(state[1], list) else state[1])
        x = jnp.swapaxes(x.reshape(x.shape[0], chips, piece, x.shape[2]), 0, 1)
        return lax.psum_scatter(x, "chip", scatter_dimension=0, tiled=False)

    def sum_second(state, *first, flops=1024):
        if not square:
            return state
        keep, send = step_call(after(scalar(second_bit), *first), *state, flops)
        return keep, flip(send, 1)

    def sum_last(state):
        return add_low(*state) if square else state[0]

    def spread_near(x):
        return jnp.stack([x, flip(x, 1)]) if square else x

    def spread_far(x):
        if not square:
            return lax.all_gather(x, "chip", axis=0, tiled=False)
        return jnp.concatenate([x, flip(x, 0)], axis=0)

    def spread_last(mine, spans, *first):
        places = []
        for c, at in ((core, slot), (1 - core, other_slot)):
            for j in range(chips):
                places.append(c * half + ((at ^ j) if square else j) * piece)
        places = after(jnp.stack(places).astype(jnp.int32), *first)
        return place_call(places, mine, other_core(mine), rows, spans)

    def in_order(bit, x, y):
        return jnp.concatenate([jnp.where(bit == 0, x, y), jnp.where(bit == 0, y, x)], axis=1)

    def my_piece(x):
        x = jnp.pad(x, ((0, 2 * half - x.shape[0]), (0, 0)))
        return lax.dynamic_slice_in_dim(x, core * half + slot * piece, piece, 0)

    def weight_near(x):
        return in_order(second_bit, x, flip(x, 1)) if square else x

    def weight_far(x, *first):
        if not square:
            x = jnp.swapaxes(lax.all_gather(x, "chip", axis=0, tiled=False), 0, 1)
            return x.reshape(x.shape[0], -1, x.shape[-1])
        return in_order(first_bit, after(x, *first) if first else x, flip(x, 0))

    def weight_rows(x):
        x = in_order(core, x, other_core(x))
        return x[:, :rows].reshape(shards * rows, x.shape[-1])

    def small_block(vectors, cols):
        x = jnp.stack(vectors).reshape(len(vectors), shards, rows)
        pad = ((0, 0), (0, SMALL_ROWS - len(vectors)), (0, cols - rows))
        return jnp.pad(jnp.swapaxes(x, 0, 1), pad)

    def with_sum(x, got):
        total = jnp.sum(got[:, :, :rows].astype(F32), axis=0).astype(BF)
        total = jnp.pad(total, ((0, 0), (0, x.shape[1] - rows)))
        row = core * half + slot * piece + lax.broadcasted_iota(jnp.int32, (piece, 1), 0)
        return jnp.where(row >= rows, total, x)[None]

    pos = (slot_index.reshape(blocks, BLK)[:, 0] // BLK).astype(jnp.int32)
    ids = jnp.arange(blocks, dtype=jnp.int32)
    tab = jnp.sum(jnp.where(pos[None, :] == ids[:, None], ids[None, :], 0), axis=1).astype(jnp.int32)
    first_len = seq_lengths[0, :1]

    hidden_own = hidden_in.T
    cot_own = cotangent.T
    small = jnp.stack(
        [attn_gain, attn_shift, query_bias, value_bias, out_bias, mlp_gain, mlp_shift, down_bias]
    )
    small = jnp.pad(small, ((0, 0), (0, 3 * wc - rows)))
    attn_piece = my_piece(attn_weight)
    parts = []
    for s in range(shards):
        cut = [window(attn_piece[:, j * width : (j + 1) * width], s) for j in range(3)]
        parts.append(jnp.concatenate([jnp.concatenate(cut, axis=1), small], axis=0))
    attn_got = exchange(jnp.stack(parts))
    small = jnp.swapaxes(attn_got[:, piece:, :rows], 0, 1).reshape(SMALL_ROWS, width)
    small = small.astype(F32).T
    hidden_all = over_shard(hidden_own)
    attn_near = after(weight_near(attn_got[:, :piece]), hidden_all)
    attn_far = weight_far(attn_near)
    normed_a, hidden = first_norm_call(tab, hidden_all, small, shards)
    w_qkv = weight_rows(after(attn_far, normed_a))
    out_piece = after(my_piece(out_weight), hidden_all)
    out_got = exchange(jnp.stack([out_piece] * shards))
    out_near = weight_near(after(out_got, attn_far))
    up_piece = after(my_piece(up_weight), out_got)
    up_got = exchange(jnp.stack([up_piece[:, s * ff_own : (s + 1) * ff_own] for s in range(shards)]))

    bias_rows = jnp.stack(
        [
            jnp.concatenate(
                [window(small[:, 2], s), jnp.zeros((wc,), F32), window(small[:, 3], s)]
            )
            for s in range(shards)
        ]
    )
    bias_qkv = after(pick(bias_rows, me)[:, None], up_got)
    qkv = (dot_tn(w_qkv, normed_a) + bias_qkv).astype(BF)
    w_out = weight_rows(weight_far(out_near, qkv))
    attended, attended_low, lse = attend(after(first_len, w_out), qkv, win)
    att_all = over_shard(attended_low)
    up_near = weight_near(after(up_got, attended_low))
    w_up = weight_rows(weight_far(after(up_near, att_all)))

    cot_all = over_shard(after(cot_own, att_all))
    att_full = jnp.concatenate([att_all[lo:hi] for lo, hi in spans], axis=0)
    middle = hidden.astype(F32) + dot_tn(w_out, att_full) + small[:, 4:5]
    average = jnp.mean(middle, axis=0, keepdims=True)
    centred = middle - average
    variance = jnp.mean(centred * centred, axis=0, keepdims=True)
    x_b = centred * lax.rsqrt(variance + EPSILON)
    normed_b = (x_b * small[:, 5:6] + small[:, 6:7]).astype(BF)
    x_b = x_b.astype(BF)

    def own_tokens(x):
        parts = [
            lax.dynamic_slice_in_dim(x, pos[me * own_blocks + j] * BLK, BLK, 1)
            for j in range(own_blocks)
        ]
        return jnp.concatenate(parts, axis=1)

    pre = dot_tn(w_up, normed_b) + up_bias.astype(F32)[:, None]
    act = gelu(pre).astype(BF)
    ffn_part = split_call(tab, dot_tn(down_weight, act).astype(BF), shards)
    ffn_chunks = ffn_part.reshape(shards, width, tok)

    def ffn_send(t, part, *first):
        return to_next(after(pick(ffn_chunks, turn(me + t))[part], *first), t)

    ffn_own = pick(ffn_chunks, me).astype(F32)
    ffn_near = ffn_send(1, slice(None))
    cot = join_blocks(after(pos, ffn_part), cot_all, shards)
    g_pre = (dot_nn(down_weight, cot) * gelu_slope(pre)).astype(BF)
    e_b = dot_nn(w_up, g_pre) + after(jnp.zeros((), F32), ffn_near)
    e_b, g_mlp_gain, g_mlp_shift = split_sums_call(tab, e_b, x_b, shards)
    ffn_own = ffn_own + ffn_near.astype(F32)
    middle_own = own_tokens(after(middle, e_b))
    g_up_bias = token_sum(after(g_pre, e_b))[:, None]

    def token_scatter(x):
        return lax.psum_scatter(x, "shard", scatter_dimension=0, tiled=True)

    e_b_own = token_scatter(e_b)
    lead = ff_own // rows
    small_down = jnp.pad(
        g_up_bias[:, 0][None, None], ((0, lead - 1), (0, SMALL_ROWS - 1), (0, width - ff_own))
    )
    down_sum = sum_start(act, cot, small_down, e_b, pieces=True)
    small_up = small_block([g_mlp_gain[:, 0], g_mlp_shift[:, 0], token_sum(cot_own)], ff_own)
    up_sum = sum_start(normed_b, g_pre, small_up, down_sum[0], pieces=True)
    merged = square and ff_own == width
    if merged:
        keep, send = first_step_call(scalar(first_bit), [down_sum, up_sum])
        ffn_sum = (keep, flip(send, 0))
    else:
        ffn_sum = (chip_sum(down_sum), chip_sum(up_sum))
    e_b_own, keep = together(e_b_own, ffn_sum[0])
    ffn_sum = (keep,) + ffn_sum[1:]

    cuts = [(lo, lo - s * wc + windows[s] * head, hi - s * wc + windows[s] * head) for s, (lo, hi) in enumerate(spans)]
    middle_grad, g_branch, sends, g_out_bias = branch_call(
        e_b_own, middle_own, cot_own, small, w_out, cuts, shards * wc
    )
    g_att = exchange(sends.reshape(shards, wc, tok)).reshape(shards * wc, tok)
    att_own = own_tokens(att_full)
    if merged:
        ffn_sum = sum_second(ffn_sum, sends)
    out_sum = sum_start(att_own, g_branch, small_block([g_out_bias[:, 0]], width), ffn_sum[0])
    keep_out = out_sum[0]
    ffn_back = ffn_send(shards - 1, slice(None), g_att)
    g_att = join_blocks(pos, g_att, shards)
    g_mixed = attend_back(first_len, qkv, g_att, attended, lse, win)
    g_mixed_rows = g_mixed.reshape(3 * wc, group)

    e_a, g_attn_gain, g_attn_shift = first_back_call(
        after(tab, keep_out, ffn_back), g_mixed_rows, hidden_all, w_qkv, shards
    )
    ffn_own = ffn_own + ffn_back.astype(F32)
    if merged:
        ffn_last = after(sum_last(ffn_sum), e_a)
        down_own, up_own = ffn_last[:lead], ffn_last[lead:]
    else:
        down_own, up_own = ffn_sum
    up_got = exchange(up_own)
    e_a_own = token_scatter(after(e_a, up_got))
    down_near = spread_near(down_own)
    up_row = with_sum(jnp.concatenate([up_got[s] for s in range(shards)], axis=-1), up_got)
    up_near = spread_near(up_row)
    cut = width // 2
    ffn_top = [ffn_send(t, slice(0, cut), e_a_own) for t in range(2, shards - 1)]
    ffn_low = [ffn_send(t, slice(cut, None), *ffn_top) for t in range(2, shards - 1)]
    for top, low in zip(ffn_top, ffn_low):
        ffn_own = ffn_own + jnp.concatenate([top, low], axis=0).astype(F32)

    def place(x):
        outs = [
            jnp.pad(x, (windows[s] * head, width - windows[s] * head - wc)) for s in range(shards)
        ]
        return pick(jnp.stack(outs), me)

    sums = jnp.sum(g_mixed.astype(F32), axis=2)
    small_mix = small_block(
        [g_attn_gain[:, 0], g_attn_shift[:, 0], place(sums[0]), place(sums[2])], 3 * wc
    )
    mix_sum = sum_start(normed_a, g_mixed_rows, small_mix)
    down_mine = spread_far(down_near)

    skip = -(-width // BLK) * BLK
    if square:
        keep, send = wide_step_call(
            after(scalar(first_bit), down_near), [(keep_out, out_sum[1]), mix_sum], (0, skip), skip + 3 * wc
        )
        wide_sum = sum_second((keep, flip(send, 0)), up_near, flops=SHORT)
        wide_own = sum_last(wide_sum)
    else:
        gap = jnp.zeros((shards, piece, skip - width), BF)
        wide_own = jnp.concatenate([chip_sum((keep_out, out_sum[1])), gap, chip_sum(mix_sum)], axis=-1)
    wide_own = after(wide_own, e_a_own, *ffn_top)
    wide_got = exchange(wide_own)
    up_mine = spread_far(after(up_near, wide_own))
    g_down_full, down_small = spread_last(down_mine, [(0, width)], wide_own)
    g_up_full, up_small = spread_last(up_mine, [(0, shards * ff_own)])
    columns = []
    for j in range(3):
        for s in range(shards):
            lo, hi = skip + j * wc + spans[s][0] - s * wc, skip + j * wc + spans[s][1] - s * wc
            columns.append(wide_got[s, :, lo:hi])
    mix_row = with_sum(jnp.concatenate(columns, axis=-1), wide_got[:, :, skip:])
    out_row = jnp.sum(wide_got[:, :, :skip].astype(F32), axis=0).astype(BF)
    wide_row = jnp.concatenate([out_row[None], mix_row], axis=-1)
    wide_near = after(spread_near(after(wide_row, g_down_full, up_mine)), *ffn_low)
    g_out_full, out_small, g_mix_full, mix_small = spread_last(
        spread_far(wide_near), [(0, width), (skip, skip + 3 * width)], g_up_full
    )

    block_out = (middle_own + ffn_own + small[:, 7:8]).astype(BF).T
    input_grad = input_call(e_a_own, hidden_own, middle_grad, small).T

    return (
        block_out,
        input_grad,
        mix_small[0, 0, :rows],
        mix_small[0, 1, :rows],
        g_mix_full[0],
        mix_small[0, 2, :rows],
        mix_small[0, 3, :rows],
        g_out_full[0],
        out_small[0, 0, :rows],
        up_small[0, 0, :rows],
        up_small[0, 1, :rows],
        g_up_full[0],
        down_small[0, 0, :ff_own],
        g_down_full.reshape(ff_own, width),
        up_small[0, 2, :rows],
    )


def solution(mesh):
    reps, shards = mesh.shape["rep"], mesh.shape["shard"]
    fine = Mesh(mesh.devices.reshape(reps // 2, 2, shards), ("chip", "core", "shard"))
    rep = ("chip", "core")
    both = ("chip", "core", "shard")
    return jax.shard_map(
        functools.partial(per_device, reps // 2, shards),
        mesh=fine,
        in_specs=(
            P(both, None),
            P(both, None),
            P(rep),
            P(rep, None),
            P("shard"),
            P("shard"),
            P("shard", None),
            P("shard"),
            P("shard"),
            P("shard", None),
            P("shard"),
            P("shard"),
            P("shard"),
            P("shard", None),
            P("shard"),
            P("shard", None),
            P("shard"),
        ),
        out_specs=(
            P(both, None),
            P(both, None),
            P("shard"),
            P("shard"),
            P("shard", None),
            P("shard"),
            P("shard"),
            P("shard", None),
            P("shard"),
            P("shard"),
            P("shard"),
            P("shard", None),
            P("shard"),
            P("shard", None),
            P("shard"),
        ),
        check_vma=False,
    )
```

```python
import functools

import jax
import jax.numpy as jnp
from jax import lax
from jax.experimental import pallas as pl
from jax.experimental.pallas import tpu as pltpu
from jax.sharding import Mesh
from jax.sharding import PartitionSpec as P

H = 25
BLK = 128
TILE = 256
EPSILON = 1e-05
BF = jnp.bfloat16
F32 = jnp.float32
VMEM_LIMIT = 56 * 1024 * 1024
SMALL_ROWS = 8


def dot_nt(a, b):
    return lax.dot_general(a, b, (((1,), (1,)), ((), ())), preferred_element_type=F32)


def dot_tn(a, b):
    return lax.dot_general(a, b, (((0,), (0,)), ((), ())), preferred_element_type=F32)


def dot_nn(a, b):
    return lax.dot_general(a, b, (((1,), (0,)), ((), ())), preferred_element_type=F32)


def head_plan(shards):
    base, extra = H // shards, H % shards
    counts = [base + (1 if s < extra else 0) for s in range(shards)]
    starts = [sum(counts[:s]) for s in range(shards)]
    width = max(counts)
    windows = [min(st, H - width) for st in starts]
    return counts, starts, windows, width


LONG = 20_000_000_000
SHORT = 10_000_000_000


def call(kernel, scalars, grid, ins, outs, scratch=(), flops=1024):
    return pl.pallas_call(
        kernel,
        out_shape=[jax.ShapeDtypeStruct(shape, dtype) for shape, dtype, _ in outs],
        grid_spec=pltpu.PrefetchScalarGridSpec(
            num_scalar_prefetch=len(scalars),
            grid=grid,
            in_specs=[spec for _, spec in ins],
            out_specs=[spec for _, _, spec in outs],
            scratch_shapes=list(scratch),
        ),
        compiler_params=pltpu.CompilerParams(vmem_limit_bytes=VMEM_LIMIT),
        cost_estimate=pl.CostEstimate(flops=flops, bytes_accessed=1024, transcendentals=0),
    )(*scalars, *[array for array, _ in ins])


def whole(array):
    zeros = (0,) * array.ndim
    return pl.BlockSpec(array.shape, lambda *_: zeros, pipeline_mode=pl.Buffered(1))


def fixed(shape):
    zeros = (0,) * len(shape)
    return pl.BlockSpec(shape, lambda *_: zeros)


def tokens(rows):
    return pl.BlockSpec((rows, TILE), lambda i, *_: (0, i))


def slot_block(rows, per, which):
    return pl.BlockSpec(
        (rows, BLK), lambda i, tab, *_: (tab[2 * i + which] // per, lax.rem(tab[2 * i + which], per))
    )


STEP = 80


def sweep(rows, body, carry, step=STEP):
    while rows % step:
        step -= 16
    for at in range(0, rows, step):
        carry = body(pl.ds(at, step), carry)
    return carry


def chunk(rows, lanes):
    step = STEP
    while rows % step:
        step -= 16
    return jnp.zeros((step, lanes), F32)


def column_mean(acc, rows):
    return jnp.sum(acc, axis=0, keepdims=True) * (1.0 / rows)


def norm_stats(load, rows, lanes):
    zero = chunk(rows, lanes)
    mean = column_mean(sweep(rows, lambda at, acc: acc + load(at), zero), rows)

    def spread(at, acc):
        centred = load(at) - mean
        return acc + centred * centred

    return mean, lax.rsqrt(column_mean(sweep(rows, spread, zero), rows) + EPSILON)


def norm_back(load, load_e, gain_ref, col, rows, lanes, write):
    mean, rstd = norm_stats(load, rows, lanes)
    zero = chunk(rows, lanes)

    def both(at):
        return (load(at) - mean) * rstd, load_e(at) * gain_ref[at, col : col + 1]

    def sums(at, carry):
        x, c = both(at)
        return carry[0] + c, carry[1] + c * x

    mean_c, mean_cx = sweep(rows, sums, (zero, zero))
    mean_c, mean_cx = column_mean(mean_c, rows), column_mean(mean_cx, rows)

    def last(at, carry):
        x, c = both(at)
        write(at, rstd * (c - mean_c - x * mean_cx))
        return carry

    sweep(rows, last, 0)


def slot_places(tab_ref, rows, per):
    places = []
    for which in range(2):
        place = tab_ref[2 * pl.program_id(0) + which]
        row = pl.multiple_of((place // per) * rows, 16)
        places.append((row, pl.multiple_of(lax.rem(place, per) * BLK, BLK)))
    return places


def store_slots(out_ref, places, at, value):
    for which, (row, lane) in enumerate(places):
        rows = pl.ds(pl.multiple_of(row + at.start, 16), at.size)
        out_ref[rows, pl.ds(lane, BLK)] = value[:, which * BLK : (which + 1) * BLK].astype(out_ref.dtype)


def clear_first(*refs):
    @pl.when(pl.program_id(0) == 0)
    def _():
        for ref in refs:
            ref[...] = jnp.zeros_like(ref)


def first_norm_kernel(tab_ref, h0_ref, h1_ref, small_ref, na_ref, pack_ref):
    rows = na_ref.shape[0]
    for j, ref in enumerate((h0_ref, h1_ref)):
        load = lambda at, ref=ref: ref[at, :].astype(F32)
        mean, rstd = norm_stats(load, rows, BLK)

        def write(at, carry, load=load, mean=mean, rstd=rstd, j=j):
            x = (load(at) - mean) * rstd
            na_ref[at, j * BLK : (j + 1) * BLK] = (x * small_ref[at, 0:1] + small_ref[at, 1:2]).astype(BF)
            return carry

        pack_ref[:, j * BLK : (j + 1) * BLK] = ref[...]

        sweep(rows, write, 0)


def first_norm_call(tab, hidden_all, small, shards):
    width, tok = small.shape[0], hidden_all.shape[1]
    group = tok * shards
    per = tok // BLK
    return call(
        first_norm_kernel,
        (tab,),
        (group // TILE,),
        [
            (hidden_all, slot_block(width, per, 0)),
            (hidden_all, slot_block(width, per, 1)),
            (small, whole(small)),
        ],
        [((width, group), BF, tokens(width))] * 2,
        flops=LONG,
    )


def tile_variants(tiles):
    return [(i, st) for i in range(tiles) for st in range(i + 1)]


def allowed_mask(first_len, q_base, k_base, k_rows):
    kpos = k_base + lax.broadcasted_iota(jnp.int32, (k_rows, TILE), 0)
    qrow = q_base + lax.broadcasted_iota(jnp.int32, (1, TILE), 1)
    low = jnp.where(qrow >= first_len, first_len, 0)
    return (kpos <= qrow) & (kpos >= low)


def attend_kernel(len_ref, q_ref, k_ref, v_ref, o_ref, ol_ref, lse_ref, *, tiles):
    first_len = len_ref[0]
    for i, st in tile_variants(tiles):
        q_base = i * TILE
        start = jnp.where(q_base >= first_len, first_len // TILE, 0)

        @pl.when(start == st)
        def _():
            rows = pl.ds(q_base, TILE)
            keys = pl.ds(st * TILE, (i + 1 - st) * TILE)
            ok = allowed_mask(first_len, q_base, st * TILE, (i + 1 - st) * TILE)
            s = dot_tn(k_ref[:, keys], q_ref[:, rows] * jnp.asarray(0.125, BF))
            s = jnp.where(ok, s, -1000000000.0)
            top = jnp.max(s, axis=0, keepdims=True)
            e = jnp.exp(s - top)
            tot = jnp.sum(e, axis=0, keepdims=True)
            soft = (e * (1.0 / tot)).astype(BF)
            o = dot_nn(v_ref[:, keys], soft)
            o_ref[:, rows] = o
            ol_ref[:, rows] = o.astype(BF)
            lse_ref[0, :, rows] = top + jnp.log(tot)


def attend(first_len, qkv, heads):
    group = qkv.shape[1]
    rows = heads * 64
    block = lambda off: pl.BlockSpec((64, group), lambda h, t, off=off: (off + h, 0))
    return call(
        functools.partial(attend_kernel, tiles=group // TILE),
        (first_len,),
        (heads,),
        [(qkv, block(0)), (qkv, block(heads)), (qkv, block(2 * heads))],
        [
            ((rows, group), F32, block(0)),
            ((rows, group), BF, block(0)),
            ((heads, 1, group), F32, pl.BlockSpec((1, 1, group), lambda h, t: (h, 0, 0))),
        ],
        flops=LONG,
    )


def attend_back_kernel(
    len_ref, q_ref, k_ref, v_ref, g_ref, o_ref, lse_ref, out_ref, dk_acc, dv_acc, *, tiles
):
    first_len = len_ref[0]
    dk_acc[...] = jnp.zeros_like(dk_acc)
    dv_acc[...] = jnp.zeros_like(dv_acc)
    for i, st in tile_variants(tiles):
        q_base = i * TILE
        start = jnp.where(q_base >= first_len, first_len // TILE, 0)

        @pl.when(start == st)
        def _():
            rows = pl.ds(q_base, TILE)
            keys = pl.ds(st * TILE, (i + 1 - st) * TILE)
            q = q_ref[:, rows] * jnp.asarray(0.125, BF)
            k = k_ref[:, keys]
            v = v_ref[:, keys]
            g = g_ref[:, rows]
            delta = jnp.sum(g.astype(F32) * o_ref[:, rows], axis=0, keepdims=True)
            ok = allowed_mask(first_len, q_base, st * TILE, (i + 1 - st) * TILE)
            s = dot_tn(k, q)
            soft = jnp.exp(jnp.where(ok, s, -1000000000.0) - lse_ref[0, :, rows])
            dp = dot_tn(v, g)
            ds = (soft * (dp - delta)).astype(BF)
            dv_acc[:, keys] += dot_nt(g, soft.astype(BF))
            dk_acc[:, keys] += dot_nt(q, ds)
            out_ref[0, :, rows] = (dot_nn(k, ds) * 0.125).astype(BF)

    out_ref[1] = dk_acc[...].astype(BF)
    out_ref[2] = dv_acc[...].astype(BF)


def attend_back(first_len, qkv, g, o, lse, heads):
    group = qkv.shape[1]
    rows = heads * 64
    block = lambda off: pl.BlockSpec((64, group), lambda h, t, off=off: (off + h, 0))
    return call(
        functools.partial(attend_back_kernel, tiles=group // TILE),
        (first_len,),
        (heads,),
        [
            (qkv, block(0)),
            (qkv, block(heads)),
            (qkv, block(2 * heads)),
            (g, block(0)),
            (o, block(0)),
            (lse, pl.BlockSpec((1, 1, group), lambda h, t: (h, 0, 0))),
        ],
        [((3, rows, group), BF, pl.BlockSpec((3, 64, group), lambda h, t: (0, h, 0)))],
        [pltpu.VMEM((64, group), F32), pltpu.VMEM((64, group), F32)],
        flops=LONG,
    )[0]


def join_kernel(pos_ref, x_ref, out):
    rows = out.shape[0]
    per = x_ref.shape[1] // BLK
    for j in range(out.shape[1] // BLK):
        at = pl.multiple_of(pos_ref[j] * BLK, BLK)
        chunk = (j // per) * rows
        out[:, pl.ds(at, BLK)] = x_ref[chunk : chunk + rows, (j % per) * BLK : (j % per + 1) * BLK]


def join_blocks(pos, x, count):
    rows, tok = x.shape[0] // count, x.shape[1]
    shape = (rows, count * tok)
    return call(join_kernel, (pos,), (1,), [(x, whole(x))], [(shape, x.dtype, fixed(shape))])[0]


def split_kernel(tab_ref, x_ref, out_ref, *, per):
    rows = x_ref.shape[0]
    store_slots(out_ref, slot_places(tab_ref, rows, per), pl.ds(0, rows), x_ref[...])


def split_call(tab, x, shards):
    width, group = x.shape
    tok = group // shards
    shape = (shards * width, tok)
    return call(
        functools.partial(split_kernel, per=tok // BLK),
        (tab,),
        (group // TILE,),
        [(x, tokens(width))],
        [(shape, BF, fixed(shape))],
    )[0]


def split_sums_kernel(tab_ref, e_ref, xb_ref, out_ref, gain_ref, shift_ref, gain_acc, shift_acc, *, per):
    clear_first(gain_acc, shift_acc)
    rows = e_ref.shape[0]
    places = slot_places(tab_ref, rows, per)

    def finish(at, carry):
        e = e_ref[at, :]
        ex = e * xb_ref[at, :].astype(F32)
        gain_acc[at, :] += ex[:, :BLK] + ex[:, BLK:]
        shift_acc[at, :] += e[:, :BLK] + e[:, BLK:]
        store_slots(out_ref, places, at, e)
        return carry

    sweep(rows, finish, 0)

    @pl.when(pl.program_id(0) == pl.num_programs(0) - 1)
    def _():
        gain_ref[...] = jnp.sum(gain_acc[...], axis=1, keepdims=True)
        shift_ref[...] = jnp.sum(shift_acc[...], axis=1, keepdims=True)


def split_sums_call(tab, e, x, shards):
    width, group = e.shape
    tok = group // shards
    shape = (shards * width, tok)
    return call(
        functools.partial(split_sums_kernel, per=tok // BLK),
        (tab,),
        (group // TILE,),
        [(e, tokens(width)), (x, tokens(width))],
        [(shape, BF, fixed(shape))] + [((width, 1), F32, fixed((width, 1)))] * 2,
        [pltpu.VMEM((width, BLK), F32), pltpu.VMEM((width, BLK), F32)],
    )


def first_back_kernel(
    tab_ref, g_ref, h0_ref, h1_ref, w_ref, ea_ref, gain_ref, shift_ref, gain_acc, shift_acc, e_ref, *, per
):
    clear_first(gain_acc, shift_acc)
    rows = w_ref.shape[0]
    e_ref[...] = dot_nn(w_ref[...], g_ref[...])
    places = slot_places(tab_ref, rows, per)
    loads = [lambda at, ref=ref: ref[at, :].astype(F32) for ref in (h0_ref, h1_ref)]
    stats = [norm_stats(load, rows, BLK) for load in loads]

    def finish(at, carry):
        e = e_ref[at, :]
        store_slots(ea_ref, places, at, e)
        total = jnp.zeros((at.size, BLK), F32)
        for j, (load, (mean, rstd)) in enumerate(zip(loads, stats)):
            total = total + e[:, j * BLK : (j + 1) * BLK] * ((load(at) - mean) * rstd)
        gain_acc[at, :] += total
        shift_acc[at, :] += e[:, :BLK] + e[:, BLK:]
        return carry

    sweep(rows, finish, 0)

    @pl.when(pl.program_id(0) == pl.num_programs(0) - 1)
    def _():
        gain_ref[...] = jnp.sum(gain_acc[...], axis=1, keepdims=True)
        shift_ref[...] = jnp.sum(shift_acc[...], axis=1, keepdims=True)


def first_back_call(tab, g_mixed, hidden_all, w, shards):
    width = w.shape[0]
    inner, group = g_mixed.shape
    tok = group // shards
    per = tok // BLK
    return call(
        functools.partial(first_back_kernel, per=per),
        (tab,),
        (group // TILE,),
        [
            (g_mixed, tokens(inner)),
            (hidden_all, slot_block(width, per, 0)),
            (hidden_all, slot_block(width, per, 1)),
            (w, whole(w)),
        ],
        [
            ((shards * width, tok), BF, fixed((shards * width, tok))),
            ((width, 1), F32, fixed((width, 1))),
            ((width, 1), F32, fixed((width, 1))),
        ],
        [pltpu.VMEM((width, BLK), F32), pltpu.VMEM((width, BLK), F32), pltpu.VMEM((width, TILE), F32)],
        flops=LONG,
    )


def branch_kernel(
    eb_ref, mid_ref, cot_ref, small_ref, w_ref, mg_ref, gb_ref, send_ref, bias_ref, att_ref, *, cuts
):
    rows, tok = mid_ref.shape

    def write(at, value):
        grad = cot_ref[at, :].astype(F32) + value
        mg_ref[at, :] = grad
        low = grad.astype(BF)
        gb_ref[at, :] = low
        bias_ref[at, :] = jnp.sum(low.astype(F32), axis=1, keepdims=True)

    norm_back(
        lambda at: mid_ref[at, :], lambda at: eb_ref[at, :].astype(F32), small_ref, 5, rows, tok, write
    )
    att_ref[...] = dot_nn(w_ref[...], gb_ref[...]).astype(BF)
    send_ref[...] = jnp.zeros_like(send_ref)
    for to, lo, hi in cuts:
        send_ref[to : to + hi - lo, :] = att_ref[lo:hi, :]


def branch_call(e_b_own, middle_own, cot_own, small, w_out, cuts, send_rows):
    width, tok = middle_own.shape
    return call(
        functools.partial(branch_kernel, cuts=cuts),
        (),
        (1,),
        [(x, whole(x)) for x in (e_b_own, middle_own, cot_own, small, w_out)],
        [
            (shape, dtype, fixed(shape))
            for shape, dtype in (
                ((width, tok), F32),
                ((width, tok), BF),
                ((send_rows, tok), BF),
                ((width, 1), F32),
            )
        ],
        [pltpu.VMEM((w_out.shape[0], tok), BF)],
    )


def input_kernel(ea_ref, h_ref, mg_ref, small_ref, out_ref):
    def write(at, value):
        out_ref[at, :] = mg_ref[at, :] + value

    rows, tok = mg_ref.shape
    norm_back(
        lambda at: h_ref[at, :].astype(F32),
        lambda at: ea_ref[at, :].astype(F32),
        small_ref,
        0,
        rows,
        tok,
        write,
    )


def input_call(e_a_own, hidden_own, middle_grad, small):
    shape = middle_grad.shape
    return call(
        input_kernel,
        (),
        (1,),
        [(x, whole(x)) for x in (e_a_own, hidden_own, middle_grad, small)],
        [(shape, F32, fixed(shape))],
    )[0]


def half_of(acc_ref, bit, count):
    return acc_ref[pl.ds(pl.multiple_of(bit * count, 8), count), :].astype(BF)


def grad_kernel(core_ref, a_ref, b_ref, small_ref, keep_ref, *refs):
    sends, acc_ref = refs[:-1], refs[-1]
    rows = a_ref.shape[0]
    count = keep_ref.shape[1]
    extra = acc_ref.shape[0] - rows - SMALL_ROWS
    acc_ref[0:rows, :] = dot_nt(a_ref[...], b_ref[...])
    acc_ref[rows : rows + SMALL_ROWS, :] = small_ref[0]
    acc_ref[rows + SMALL_ROWS :, :] = jnp.zeros((extra, acc_ref.shape[1]), F32)
    keep_ref[0] = half_of(acc_ref, core_ref[0], count)
    if len(sends) == 1:
        sends[0][0] = half_of(acc_ref, 1 - core_ref[0], count)
        return
    for n, send_ref in enumerate(sends):

        @pl.when(pl.program_id(0) == n)
        def _(send_ref=send_ref):
            send_ref[...] = half_of(acc_ref, 1 - core_ref[0], count)


def grad_call(core, a, b, small, half, pieces):
    lead, _, cols = small.shape
    rows, group = a.shape[0] // lead, a.shape[1]
    keep = ((lead, half, cols), BF, pl.BlockSpec((1, half, cols), lambda i, *_: (i, 0, 0)))
    outs = call(
        grad_kernel,
        (core,),
        (lead,),
        [
            (a, pl.BlockSpec((rows, group), lambda i, *_: (i, 0))),
            (b, whole(b)),
            (small, pl.BlockSpec((1, SMALL_ROWS, cols), lambda i, *_: (i, 0, 0))),
        ],
        [keep] + ([((half, cols), BF, fixed((half, cols)))] * lead if pieces else [keep]),
        [pltpu.VMEM((2 * half, cols), F32)],
    )
    return outs[0], outs[1:] if pieces else outs[1]


def first_step_kernel(bit_ref, *refs, leads):
    ins, (keep_ref, send_ref, acc_ref) = refs[:-3], refs[-3:]
    count = keep_ref.shape[1]
    first = at = 0
    for lead in leads:
        for n in range(lead):

            @pl.when(pl.program_id(0) == first + n)
            def _(x_ref=ins[at], y_ref=ins[at + 1 + n]):
                acc_ref[...] = x_ref[0].astype(F32) + y_ref[...].astype(F32)

        first += lead
        at += 1 + lead
    keep_ref[0] = half_of(acc_ref, bit_ref[0], count)
    send_ref[0] = half_of(acc_ref, 1 - bit_ref[0], count)


def first_step_call(bit, sums):
    _, count, cols = sums[0][0].shape
    leads = [x.shape[0] for x, _ in sums]
    total = sum(leads)
    ins = []
    first = 0
    for (x, pieces), lead in zip(sums, leads):
        at = lambda i, *_, first=first, lead=lead: (jnp.clip(i - first, 0, lead - 1), 0, 0)
        ins.append((x, pl.BlockSpec((1, count, cols), at)))
        ins += [(y, whole(y)) for y in pieces]
        first += lead
    part = ((total, count // 2, cols), BF, pl.BlockSpec((1, count // 2, cols), lambda i, *_: (i, 0, 0)))
    return call(
        functools.partial(first_step_kernel, leads=leads),
        (bit,),
        (total,),
        ins,
        [part, part],
        [pltpu.VMEM((count, cols), F32)],
    )


def wide_step_kernel(bit_ref, *refs, wide):
    ins, (keep_ref, send_ref, acc_ref) = refs[:-3], refs[-3:]
    count = keep_ref.shape[1]
    end = 0
    for n, (lo, hi) in enumerate(wide):
        if lo > end:
            acc_ref[:, end:lo] = jnp.zeros((acc_ref.shape[0], lo - end), F32)
        end = hi
        acc_ref[:, lo:hi] = ins[2 * n][0].astype(F32) + ins[2 * n + 1][0].astype(F32)
    keep_ref[0] = half_of(acc_ref, bit_ref[0], count)
    send_ref[0] = half_of(acc_ref, 1 - bit_ref[0], count)


def wide_step_call(bit, sums, offsets, cols):
    lead, count, _ = sums[0][0].shape
    ins, wide = [], []
    for (x, y), lo in zip(sums, offsets):
        wide.append((lo, lo + x.shape[2]))
        ins += [(z, pl.BlockSpec((1, count, z.shape[2]), lambda i, *_: (i, 0, 0))) for z in (x, y)]
    part = ((lead, count // 2, cols), BF, pl.BlockSpec((1, count // 2, cols), lambda i, *_: (i, 0, 0)))
    return call(
        functools.partial(wide_step_kernel, wide=wide),
        (bit,),
        (lead,),
        ins,
        [part, part],
        [pltpu.VMEM((count, cols), F32)],
        flops=SHORT,
    )


def step_kernel(bit_ref, x_ref, y_ref, keep_ref, send_ref, acc_ref):
    count = keep_ref.shape[1]
    acc_ref[...] = x_ref[0].astype(F32) + y_ref[0].astype(F32)
    keep_ref[0] = half_of(acc_ref, bit_ref[0], count)
    send_ref[0] = half_of(acc_ref, 1 - bit_ref[0], count)


def step_call(bit, x, y, flops):
    lead, count, cols = x.shape
    block = pl.BlockSpec((1, count, cols), lambda i, *_: (i, 0, 0))
    part = ((lead, count // 2, cols), BF, pl.BlockSpec((1, count // 2, cols), lambda i, *_: (i, 0, 0)))
    return call(
        step_kernel, (bit,), (lead,), [(x, block), (y, block)], [part, part], [pltpu.VMEM((count, cols), F32)], flops
    )


def place_kernel(at_ref, mine_ref, theirs_ref, *refs, spans):
    outs, acc_ref = refs[:-1], refs[-1]
    pieces, _, count, _ = mine_ref.shape
    rows = outs[0].shape[1]
    for n in range(2 * pieces):
        at = pl.multiple_of(at_ref[n], 8)
        acc_ref[pl.ds(at, count), :] = (theirs_ref if n >= pieces else mine_ref)[n % pieces, 0].astype(F32)
    for n, (lo, hi) in enumerate(spans):
        outs[2 * n][0] = acc_ref[0:rows, lo:hi]
        outs[2 * n + 1][0] = acc_ref[rows : rows + SMALL_ROWS, lo:hi]


def place_call(places, mine, theirs, rows, spans):
    pieces, lead, count, cols = mine.shape
    cut = 1280 if cols % 1280 == 0 and len(spans) == 1 else cols
    block = pl.BlockSpec((pieces, 1, count, cut), lambda i, j, *_: (0, i, 0, j))
    outs = []
    for lo, hi in spans:
        lanes = min(hi - lo, cut)
        for height in (rows, SMALL_ROWS):
            spec = pl.BlockSpec((1, height, lanes), lambda i, j, *_: (i, 0, j))
            outs.append(((lead, height, hi - lo), F32, spec))
    inner = [(0, cut)] if len(spans) == 1 else spans
    return call(
        functools.partial(place_kernel, spans=inner),
        (places,),
        (lead, cols // cut),
        [(mine, block), (theirs, block)],
        outs,
        [pltpu.VMEM((2 * pieces * count, cut), F32)],
        flops=SHORT,
    )


ROOT = 0.7978845608028654
CUBE = 0.044715


def gelu(u):
    return 0.5 * u * (1.0 + jnp.tanh(ROOT * (u + CUBE * u * u * u)))


def gelu_slope(u):
    bend = jnp.tanh(ROOT * (u + CUBE * u * u * u))
    return 0.5 * (1.0 + bend) + 0.5 * u * (1.0 - bend * bend) * (ROOT * (1.0 + 3.0 * CUBE * u * u))


def token_sum(values_in):
    return jnp.sum(values_in.astype(F32), axis=1)


def after(x, *first):
    return lax.optimization_barrier((x,) + first)[0]


def together(*values):
    return lax.optimization_barrier(values)


def per_device(
    chips,
    shards,
    hidden_in,
    cotangent,
    slot_index,
    seq_lengths,
    attn_gain,
    attn_shift,
    attn_weight,
    query_bias,
    value_bias,
    out_weight,
    out_bias,
    mlp_gain,
    mlp_shift,
    up_weight,
    up_bias,
    down_weight,
    down_bias,
):
    tok, width = hidden_in.shape
    group = slot_index.shape[0]
    head = width // H
    rows = width // shards
    ff_own = down_weight.shape[0]
    counts, starts, windows, win = head_plan(shards)
    wc = win * head
    reps = 2 * chips
    piece = -(-(rows + SMALL_ROWS) // (8 * reps)) * 8
    half = chips * piece
    me = lax.axis_index("shard")
    chip = lax.axis_index("chip")
    core = lax.axis_index("core")
    blocks = group // BLK
    own_blocks = tok // BLK
    spans = []
    for s in range(shards):
        lo = (starts[s] - windows[s]) * head
        spans.append((s * wc + lo, s * wc + lo + counts[s] * head))

    def to_next(x, t):
        return lax.ppermute(x, "shard", [(i, (i + t) % shards) for i in range(shards)])

    def other_core(x):
        return lax.ppermute(x, "core", [(0, 1), (1, 0)])

    def pick(x, at):
        return lax.dynamic_index_in_dim(x, at, 0, keepdims=False)

    def turn(j):
        return lax.rem(j + 2 * shards, shards)

    def exchange(send):
        got = [pick(send, me)]
        for t in range(1, shards):
            got.append(to_next(pick(send, turn(me + t)), t))
        got = jnp.stack(got)
        return jnp.stack([pick(got, turn(me - j)) for j in range(shards)])

    def over_shard(x):
        return lax.all_gather(x, "shard", axis=0, tiled=True)

    def window(x, s):
        return x[..., windows[s] * head : windows[s] * head + wc]

    def scalar(x):
        return jnp.reshape(x, (1,)).astype(jnp.int32)

    square = chips == 4
    bits = (chip // 2, chip % 2)
    first_bit = jnp.where(core == 0, bits[1], bits[0])
    second_bit = jnp.where(core == 0, bits[0], bits[1])
    slot = 2 * first_bit + second_bit if square else chip
    other_slot = 2 * second_bit + first_bit

    def flip(x, step):
        pairs = []
        for q in range(chips):
            for c in range(2):
                partner = q ^ 1 if (c + step) % 2 == 0 else q ^ 2
                pairs.append((2 * q + c, 2 * partner + c))
        return lax.ppermute(x, ("chip", "core"), pairs)

    def add_low(x, y):
        return (x.astype(F32) + y.astype(F32)).astype(BF)

    def sum_start(a, b, small, *first, pieces=False):
        keep, sends = grad_call(after(scalar(core), *first), a, b, small, half, pieces)
        return keep, [other_core(x) for x in sends] if pieces else other_core(sends)

    def chip_sum(state):
        x = add_low(state[0], jnp.stack(state[1]) if isinstance(state[1], list) else state[1])
        x = jnp.swapaxes(x.reshape(x.shape[0], chips, piece, x.shape[2]), 0, 1)
        return lax.psum_scatter(x, "chip", scatter_dimension=0, tiled=False)

    def sum_second(state, *first, flops=1024):
        if not square:
            return state
        keep, send = step_call(after(scalar(second_bit), *first), *state, flops)
        return keep, flip(send, 1)

    def sum_last(state):
        return add_low(*state) if square else state[0]

    def spread_near(x):
        return jnp.stack([x, flip(x, 1)]) if square else x

    def spread_far(x):
        if not square:
            return lax.all_gather(x, "chip", axis=0, tiled=False)
        return jnp.concatenate([x, flip(x, 0)], axis=0)

    def spread_last(mine, spans, *first):
        places = []
        for c, at in ((core, slot), (1 - core, other_slot)):
            for j in range(chips):
                places.append(c * half + ((at ^ j) if square else j) * piece)
        places = after(jnp.stack(places).astype(jnp.int32), *first)
        return place_call(places, mine, other_core(mine), rows, spans)

    def in_order(bit, x, y):
        return jnp.concatenate([jnp.where(bit == 0, x, y), jnp.where(bit == 0, y, x)], axis=1)

    def my_piece(x):
        x = jnp.pad(x, ((0, 2 * half - x.shape[0]), (0, 0)))
        return lax.dynamic_slice_in_dim(x, core * half + slot * piece, piece, 0)

    def weight_near(x):
        return in_order(second_bit, x, flip(x, 1)) if square else x

    def weight_far(x, *first):
        if not square:
            x = jnp.swapaxes(lax.all_gather(x, "chip", axis=0, tiled=False), 0, 1)
            return x.reshape(x.shape[0], -1, x.shape[-1])
        return in_order(first_bit, after(x, *first) if first else x, flip(x, 0))

    def weight_rows(x):
        x = in_order(core, x, other_core(x))
        return x[:, :rows].reshape(shards * rows, x.shape[-1])

    def small_block(vectors, cols):
        x = jnp.stack(vectors).reshape(len(vectors), shards, rows)
        pad = ((0, 0), (0, SMALL_ROWS - len(vectors)), (0, cols - rows))
        return jnp.pad(jnp.swapaxes(x, 0, 1), pad)

    def with_sum(x, got):
        total = jnp.sum(got[:, :, :rows].astype(F32), axis=0).astype(BF)
        total = jnp.pad(total, ((0, 0), (0, x.shape[1] - rows)))
        row = core * half + slot * piece + lax.broadcasted_iota(jnp.int32, (piece, 1), 0)
        return jnp.where(row >= rows, total, x)[None]

    pos = (slot_index.reshape(blocks, BLK)[:, 0] // BLK).astype(jnp.int32)
    ids = jnp.arange(blocks, dtype=jnp.int32)
    tab = jnp.sum(jnp.where(pos[None, :] == ids[:, None], ids[None, :], 0), axis=1).astype(jnp.int32)
    first_len = seq_lengths[0, :1]

    hidden_own = hidden_in.T
    cot_own = cotangent.T
    small = jnp.stack(
        [attn_gain, attn_shift, query_bias, value_bias, out_bias, mlp_gain, mlp_shift, down_bias]
    )
    small = jnp.pad(small, ((0, 0), (0, 3 * wc - rows)))
    attn_piece = my_piece(attn_weight)
    parts = []
    for s in range(shards):
        cut = [window(attn_piece[:, j * width : (j + 1) * width], s) for j in range(3)]
        parts.append(jnp.concatenate([jnp.concatenate(cut, axis=1), small], axis=0))
    attn_got = exchange(jnp.stack(parts))
    small = jnp.swapaxes(attn_got[:, piece:, :rows], 0, 1).reshape(SMALL_ROWS, width)
    small = small.astype(F32).T
    hidden_all = over_shard(hidden_own)
    attn_near = after(weight_near(attn_got[:, :piece]), hidden_all)
    attn_far = weight_far(attn_near)
    normed_a, hidden = first_norm_call(tab, hidden_all, small, shards)
    w_qkv = weight_rows(after(attn_far, normed_a))
    out_piece = after(my_piece(out_weight), hidden_all)
    out_got = exchange(jnp.stack([out_piece] * shards))
    out_near = weight_near(after(out_got, attn_far))
    up_piece = after(my_piece(up_weight), out_got)
    up_got = exchange(jnp.stack([up_piece[:, s * ff_own : (s + 1) * ff_own] for s in range(shards)]))

    bias_rows = jnp.stack(
        [
            jnp.concatenate(
                [window(small[:, 2], s), jnp.zeros((wc,), F32), window(small[:, 3], s)]
            )
            for s in range(shards)
        ]
    )
    bias_qkv = after(pick(bias_rows, me)[:, None], up_got)
    qkv = (dot_tn(w_qkv, normed_a) + bias_qkv).astype(BF)
    w_out = weight_rows(weight_far(out_near, qkv))
    attended, attended_low, lse = attend(after(first_len, w_out), qkv, win)
    att_all = over_shard(attended_low)
    up_near = weight_near(after(up_got, attended_low))
    w_up = weight_rows(weight_far(after(up_near, att_all)))

    cot_all = over_shard(after(cot_own, att_all))
    att_full = jnp.concatenate([att_all[lo:hi] for lo, hi in spans], axis=0)
    middle = hidden.astype(F32) + dot_tn(w_out, att_full) + small[:, 4:5]
    average = jnp.mean(middle, axis=0, keepdims=True)
    centred = middle - average
    variance = jnp.mean(centred * centred, axis=0, keepdims=True)
    x_b = centred * lax.rsqrt(variance + EPSILON)
    normed_b = (x_b * small[:, 5:6] + small[:, 6:7]).astype(BF)
    x_b = x_b.astype(BF)

    def own_tokens(x):
        parts = [
            lax.dynamic_slice_in_dim(x, pos[me * own_blocks + j] * BLK, BLK, 1)
            for j in range(own_blocks)
        ]
        return jnp.concatenate(parts, axis=1)

    pre = dot_tn(w_up, normed_b) + up_bias.astype(F32)[:, None]
    act = gelu(pre).astype(BF)
    ffn_part = split_call(tab, dot_tn(down_weight, act).astype(BF), shards)
    ffn_chunks = ffn_part.reshape(shards, width, tok)

    def ffn_send(t, part, *first):
        return to_next(after(pick(ffn_chunks, turn(me + t))[part], *first), t)

    ffn_own = pick(ffn_chunks, me).astype(F32)
    ffn_near = ffn_send(1, slice(None))
    cot = join_blocks(after(pos, ffn_part), cot_all, shards)
    g_pre = (dot_nn(down_weight, cot) * gelu_slope(pre)).astype(BF)
    e_b = dot_nn(w_up, g_pre) + after(jnp.zeros((), F32), ffn_near)
    e_b, g_mlp_gain, g_mlp_shift = split_sums_call(tab, e_b, x_b, shards)
    ffn_own = ffn_own + ffn_near.astype(F32)
    middle_own = own_tokens(after(middle, e_b))
    g_up_bias = token_sum(after(g_pre, e_b))[:, None]

    def token_scatter(x):
        return lax.psum_scatter(x, "shard", scatter_dimension=0, tiled=True)

    e_b_own = token_scatter(e_b)
    lead = ff_own // rows
    small_down = jnp.pad(
        g_up_bias[:, 0][None, None], ((0, lead - 1), (0, SMALL_ROWS - 1), (0, width - ff_own))
    )
    down_sum = sum_start(act, cot, small_down, e_b, pieces=True)
    small_up = small_block([g_mlp_gain[:, 0], g_mlp_shift[:, 0], token_sum(cot_own)], ff_own)
    up_sum = sum_start(normed_b, g_pre, small_up, down_sum[0], pieces=True)
    merged = square and ff_own == width
    if merged:
        keep, send = first_step_call(scalar(first_bit), [down_sum, up_sum])
        ffn_sum = (keep, flip(send, 0))
    else:
        ffn_sum = (chip_sum(down_sum), chip_sum(up_sum))
    e_b_own, keep = together(e_b_own, ffn_sum[0])
    ffn_sum = (keep,) + ffn_sum[1:]

    cuts = [(lo, lo - s * wc + windows[s] * head, hi - s * wc + windows[s] * head) for s, (lo, hi) in enumerate(spans)]
    middle_grad, g_branch, sends, g_out_bias = branch_call(
        e_b_own, middle_own, cot_own, small, w_out, cuts, shards * wc
    )
    g_att = exchange(sends.reshape(shards, wc, tok)).reshape(shards * wc, tok)
    att_own = own_tokens(att_full)
    if merged:
        ffn_sum = sum_second(ffn_sum, sends)
    out_sum = sum_start(att_own, g_branch, small_block([g_out_bias[:, 0]], width), ffn_sum[0])
    keep_out = out_sum[0]
    ffn_back = ffn_send(shards - 1, slice(None), g_att)
    g_att = join_blocks(pos, g_att, shards)
    g_mixed = attend_back(first_len, qkv, g_att, attended, lse, win)
    g_mixed_rows = g_mixed.reshape(3 * wc, group)

    e_a, g_attn_gain, g_attn_shift = first_back_call(
        after(tab, keep_out, ffn_back), g_mixed_rows, hidden_all, w_qkv, shards
    )
    ffn_own = ffn_own + ffn_back.astype(F32)
    if merged:
        ffn_last = after(sum_last(ffn_sum), e_a)
        down_own, up_own = ffn_last[:lead], ffn_last[lead:]
    else:
        down_own, up_own = ffn_sum
    up_got = exchange(up_own)
    e_a_own = token_scatter(after(e_a, up_got))
    down_near = spread_near(down_own)
    up_row = with_sum(jnp.concatenate([up_got[s] for s in range(shards)], axis=-1), up_got)
    up_near = spread_near(up_row)
    cut = width // 2
    ffn_top = [ffn_send(t, slice(0, cut), e_a_own) for t in range(2, shards - 1)]
    ffn_low = [ffn_send(t, slice(cut, None), *ffn_top) for t in range(2, shards - 1)]
    for top, low in zip(ffn_top, ffn_low):
        ffn_own = ffn_own + jnp.concatenate([top, low], axis=0).astype(F32)

    def place(x):
        outs = [
            jnp.pad(x, (windows[s] * head, width - windows[s] * head - wc)) for s in range(shards)
        ]
        return pick(jnp.stack(outs), me)

    sums = jnp.sum(g_mixed.astype(F32), axis=2)
    small_mix = small_block(
        [g_attn_gain[:, 0], g_attn_shift[:, 0], place(sums[0]), place(sums[2])], 3 * wc
    )
    mix_sum = sum_start(normed_a, g_mixed_rows, small_mix)

    skip = -(-width // BLK) * BLK
    if square:
        keep, send = wide_step_call(
            after(scalar(first_bit), down_near), [(keep_out, out_sum[1]), mix_sum], (0, skip), skip + 3 * wc
        )
        wide_sum = sum_second((keep, flip(send, 0)), up_near, flops=SHORT)
        wide_own = sum_last(wide_sum)
    else:
        gap = jnp.zeros((shards, piece, skip - width), BF)
        wide_own = jnp.concatenate([chip_sum((keep_out, out_sum[1])), gap, chip_sum(mix_sum)], axis=-1)
    wide_own = after(wide_own, e_a_own, *ffn_top)
    wide_got = exchange(wide_own)
    up_mine = spread_far(after(up_near, wide_own))
    down_mine = spread_far(after(down_near, wide_own))
    g_down_full, down_small = spread_last(down_mine, [(0, width)])
    g_up_full, up_small = spread_last(up_mine, [(0, shards * ff_own)])
    columns = []
    for j in range(3):
        for s in range(shards):
            lo, hi = skip + j * wc + spans[s][0] - s * wc, skip + j * wc + spans[s][1] - s * wc
            columns.append(wide_got[s, :, lo:hi])
    mix_row = with_sum(jnp.concatenate(columns, axis=-1), wide_got[:, :, skip:])
    out_row = jnp.sum(wide_got[:, :, :skip].astype(F32), axis=0).astype(BF)
    wide_row = jnp.concatenate([out_row[None], mix_row], axis=-1)
    wide_near = spread_near(after(wide_row, up_mine))
    g_out_full, out_small, g_mix_full, mix_small = spread_last(
        spread_far(wide_near), [(0, width), (skip, skip + 3 * width)], g_up_full, g_down_full, *ffn_low
    )

    block_out = (middle_own + ffn_own + small[:, 7:8]).astype(BF).T
    input_grad = input_call(e_a_own, hidden_own, middle_grad, small).T

    return (
        block_out,
        input_grad,
        mix_small[0, 0, :rows],
        mix_small[0, 1, :rows],
        g_mix_full[0],
        mix_small[0, 2, :rows],
        mix_small[0, 3, :rows],
        g_out_full[0],
        out_small[0, 0, :rows],
        up_small[0, 0, :rows],
        up_small[0, 1, :rows],
        g_up_full[0],
        down_small[0, 0, :ff_own],
        g_down_full.reshape(ff_own, width),
        up_small[0, 2, :rows],
    )


def solution(mesh):
    reps, shards = mesh.shape["rep"], mesh.shape["shard"]
    fine = Mesh(mesh.devices.reshape(reps // 2, 2, shards), ("chip", "core", "shard"))
    rep = ("chip", "core")
    both = ("chip", "core", "shard")
    return jax.shard_map(
        functools.partial(per_device, reps // 2, shards),
        mesh=fine,
        in_specs=(
            P(both, None),
            P(both, None),
            P(rep),
            P(rep, None),
            P("shard"),
            P("shard"),
            P("shard", None),
            P("shard"),
            P("shard"),
            P("shard", None),
            P("shard"),
            P("shard"),
            P("shard"),
            P("shard", None),
            P("shard"),
            P("shard", None),
            P("shard"),
        ),
        out_specs=(
            P(both, None),
            P(both, None),
            P("shard"),
            P("shard"),
            P("shard", None),
            P("shard"),
            P("shard"),
            P("shard", None),
            P("shard"),
            P("shard"),
            P("shard"),
            P("shard", None),
            P("shard"),
            P("shard", None),
            P("shard"),
        ),
        check_vma=False,
    )
```
